128 devices in a mesh: blk: 16 (over x, y_hi, core), head: 8 (over y_lo, z).
Axes of the slice: x: 4, y: 4 (y_hi: 2, y_lo: 2; y = y_hi * 2 + y_lo), z: 4, core: 2. Of those that a mesh axis runs over, the one named last changes fastest.
Arguments:
- queries: bfloat16 [16384, 3072], P(('blk', 'head')), may hold values from -8 to 8
- keys: bfloat16 [16384, 3072], P(('blk', 'head')), may hold values from -8 to 8
- values: bfloat16 [16384, 3072], P(('blk', 'head')), may hold values from -6 to 6
- d_queries: bfloat16 [16384, 3072], P(('blk', 'head')), may hold values from -6 to 6
- d_keys: bfloat16 [16384, 3072], P(('blk', 'head')), may hold values from -6 to 6
- d_values: bfloat16 [16384, 3072], P(('blk', 'head')), may hold values from -6 to 6
- positions: int32 [3, 16384], P(None, ('blk', 'head')), may hold values from 0 to 79, as said below
- key_lists: int32 [16, 5], replicated, may hold values from -1 to 15, as said below
Outputs:
- attended: bfloat16 [16384, 3072], P(('blk', 'head'))
- d_attended: bfloat16 [16384, 3072], P(('blk', 'head'))
The draws below stay inside these ranges and needn't reach their ends.
Inputs may be any that keep to these rules, and one draw needn't show every extreme that they name: `key_lists`: row r lists between 1 and 5 different key blocks, each within 3 of r, always r itself, nearer blocks more often; unused slots are -1 and come last; some row lists exactly 5 blocks. `positions`: frame indices are below 21, height indices below 45, width indices below 80.
All inputs are finite; a program needn't handle non-finite values.
Results may differ from the reference program's by a relative error of at most 0.018.
Values may be sent and summed in bfloat16 or wider, within the bound.
A program may use at most 192 MiB of HBM per device.

```python
import jax
import jax.numpy as jnp
import numpy as np
from jax import lax

HEADS = 24
HEAD_DIM = 128
REACH = 3
MOST = 5
QB = 1024
TOKENS = 16384
N_BLK = 16


def token_positions(key):
    first, second, third = jax.random.split(key, 3)
    frames = jax.random.randint(first, (TOKENS,), 0, 21)
    height = jax.random.randint(second, (TOKENS,), 0, 45)
    width = jax.random.randint(third, (TOKENS,), 0, 80)
    return jnp.stack([frames, height, width]).astype(jnp.int32)


def draw_positions(key, part):
    return token_positions(key)


def draw_queries(key, part):
    key = jax.random.fold_in(key, 21)
    base = jnp.clip(jax.random.normal(key, (TOKENS, HEADS * 128), jnp.float32), -4.0, 4.0)
    return base.astype(jnp.bfloat16)


def draw_keys(key, part):
    key = jax.random.fold_in(key, 31)
    base = jnp.clip(jax.random.normal(key, (TOKENS, HEADS * 128), jnp.float32), -4.0, 4.0)
    return base.astype(jnp.bfloat16)


def draw_key_lists(key, part):
    key = jax.random.fold_in(key, 5)
    offsets_list = [0]
    for distance in range(1, REACH + 1):
        offsets_list = offsets_list + [-distance, distance]
    offsets = jnp.array(offsets_list, jnp.int32)
    width = len(offsets_list)
    blocks = jnp.arange(N_BLK, dtype=jnp.int32)[:, None] + offsets[None, :]
    valid = (blocks >= 0) & (blocks < N_BLK)
    first, second, third = jax.random.split(key, 3)
    jitter = jax.random.randint(first, (N_BLK, width), 0, width)
    priority = jnp.abs(offsets)[None, :] * width * width + jitter * width + jnp.arange(width, dtype=jnp.int32)[None, :]
    priority = jnp.where(valid, priority, 1000000)
    order = jnp.argsort(priority, axis=1, stable=True)
    ranked = jnp.take_along_axis(blocks, order, axis=1)
    available = jnp.sum(valid.astype(jnp.int32), axis=1)
    count = jax.random.randint(second, (N_BLK,), 1, MOST + 1)
    forced = jax.random.randint(third, (), REACH, N_BLK - REACH)
    count = jnp.where(jnp.arange(N_BLK) == forced, MOST, count)
    count = jnp.minimum(count, available)
    slots = jnp.arange(MOST, dtype=jnp.int32)[None, :]
    return jnp.where(slots < count[:, None], ranked[:, :MOST], -1).astype(jnp.int32)


def shard_levels(own_key, shape, pieces, smallest, high):
    def one(position, parts):
        heights = jax.random.uniform(jax.random.fold_in(jax.random.fold_in(own_key, 6), position), (parts,), jnp.float32, smallest / len(pieces), high / len(pieces))
        return jnp.repeat(jnp.exp(heights), shape[position] // parts).reshape((-1,) + (1,) * (len(shape) - position - 1))

    factor_of = one(*pieces[0])
    for cut in pieces[1:]:
        factor_of = factor_of * one(*cut)
    return factor_of


def centred(key, extent, scale, limit, cuts=(), held_as=jnp.bfloat16):
    result = scale * jax.random.normal(key, extent, jnp.float32)
    if cuts:
        result = result * shard_levels(key, extent, cuts, -0.22, 0.18)
    return jnp.clip(result, -limit, limit).astype(held_as)


def setup_inputs(seed: int = 0) -> dict:
    key_of = jax.random.split(jax.random.key(seed), 9)
    return {
        "queries": draw_queries(jax.random.fold_in(key_of[8], 71), 0),
        "keys": draw_keys(jax.random.fold_in(key_of[8], 71), 0),
        "values": centred(key_of[2], (TOKENS, HEADS * HEAD_DIM), 1.0, 6.0, ((0, 128),)),
        "d_queries": centred(key_of[3], (TOKENS, HEADS * HEAD_DIM), 1.0, 6.0, ((0, 128),)),
        "d_keys": centred(key_of[4], (TOKENS, HEADS * HEAD_DIM), 1.0, 6.0, ((0, 128),)),
        "d_values": centred(key_of[5], (TOKENS, HEADS * HEAD_DIM), 1.0, 6.0, ((0, 128),)),
        "positions": draw_positions(jax.random.fold_in(key_of[8], 71), 0),
        "key_lists": draw_key_lists(jax.random.fold_in(key_of[8], 71), 0),
    }


def frequency_rows():
    tables = np.zeros((3, 128), np.float32)
    start = 0
    for axis_id, count, span in ((0, 22, 44), (1, 21, 42), (2, 21, 42)):
        for column in range(count):
            rate = 1.0 / (10000.0 ** (2.0 * column / span))
            tables[axis_id, 2 * (start + column)] = rate
            tables[axis_id, 2 * (start + column) + 1] = rate
        start += count
    return tables


def swap_table():
    table = np.zeros((128, 128), np.float32)
    for pair in range(64):
        table[2 * pair + 1, 2 * pair] = -1.0
        table[2 * pair, 2 * pair + 1] = 1.0
    return table


def rotate(tokens_in, positions):
    count = tokens_in.shape[0]
    heads = tokens_in.shape[1] // 128
    rates = jnp.asarray(frequency_rows(), jnp.float32)
    spots = positions.astype(jnp.float32)
    angle = spots[0][:, None] * rates[0] + spots[1][:, None] * rates[1] + spots[2][:, None] * rates[2]
    cosine = jnp.cos(angle)[:, None, :]
    sine = jnp.sin(angle)[:, None, :]
    shaped = tokens_in.reshape(count, heads, 128).astype(jnp.float32)
    swapped = jnp.einsum("nhd,de->nhe", shaped, jnp.asarray(swap_table(), jnp.float32), precision=lax.Precision.HIGHEST)
    return (shaped * cosine + swapped * sine).astype(jnp.bfloat16).reshape(count, heads * 128)


def reference(queries, keys, values, d_queries, d_keys, d_values, positions, key_lists):
    scale = HEAD_DIM ** -0.5
    high = lax.Precision.HIGHEST

    def heads_first(array):
        array = lax.optimization_barrier(array)
        return array.reshape(N_BLK, QB, HEADS, HEAD_DIM).transpose(2, 0, 1, 3)

    query_all = heads_first(rotate(queries, positions))
    key_all = heads_first(rotate(keys, positions))
    dquery_all = heads_first(rotate(d_queries, positions))
    dkey_all = heads_first(rotate(d_keys, positions))
    value_all = heads_first(values)
    dvalue_all = heads_first(d_values)

    def per_block(index):
        row = key_lists[index]
        live = row >= 0
        safe = jnp.maximum(row, 0).astype(jnp.int32)
        mask = jnp.repeat(live, QB)

        def per_head(head):
            def pick(array):
                return array[head][safe].reshape(MOST * QB, HEAD_DIM).astype(jnp.float32)

            query = query_all[head, index].astype(jnp.float32)
            dquery = dquery_all[head, index].astype(jnp.float32)
            keyset = pick(key_all)
            dkeyset = pick(dkey_all)
            valueset = pick(value_all)
            dvalueset = pick(dvalue_all)
            score = jnp.dot(query, keyset.T, precision=high) * scale
            d_score = (jnp.dot(dquery, keyset.T, precision=high) + jnp.dot(query, dkeyset.T, precision=high)) * scale
            score = jnp.where(mask[None, :], score, -1e30)
            top = jnp.max(score, axis=1)
            weight = jnp.exp(score - top[:, None])
            tilted_full = weight * d_score
            total = jnp.sum(weight, axis=1)
            slope = jnp.sum(tilted_full, axis=1)
            light = lax.optimization_barrier(weight.astype(jnp.bfloat16)).astype(jnp.float32)
            tilted = lax.optimization_barrier(tilted_full.astype(jnp.bfloat16)).astype(jnp.float32)
            output = jnp.dot(light, valueset, precision=high) / total[:, None]
            d_output = (jnp.dot(light, dvalueset, precision=high) + jnp.dot(tilted, valueset, precision=high)) / total[:, None]
            d_output = d_output - (slope / total)[:, None] * output
            return output.astype(jnp.bfloat16), d_output.astype(jnp.bfloat16)

        return lax.map(per_head, jnp.arange(HEADS))

    outputs, d_outputs = lax.map(per_block, jnp.arange(N_BLK))
    attended = outputs.transpose(0, 2, 1, 3).reshape(TOKENS, HEADS * HEAD_DIM)
    d_attended = d_outputs.transpose(0, 2, 1, 3).reshape(TOKENS, HEADS * HEAD_DIM)
    return attended, d_attended
```

```python
import functools

import jax
import jax.numpy as jnp
import numpy as np
from jax import lax
from jax.experimental import pallas as pl
from jax.experimental.pallas import tpu as pltpu
from jax.sharding import PartitionSpec as P

MESH = pl.DeviceIdType.MESH
REACH = 3
BLOCKS = 16
CHUNK = 128
QB = 1024
SCALE = 128 ** (-0.5)
LOG2E = 1.4426950408889634
CHIP_X = (0, 2, 3, 1, 2, 0, 1, 3)
SLOTS = 12
ORDER = (0, 5, 2, 3, 1, 4)


def chip_runs():
    runs = []
    for k in range(8):
        mine, base = [], 0
        for j in range(3):
            blocks = [job % 16 for job in range(6 * k, 6 * k + 6) if job // 16 == j]
            if blocks:
                low, high = max(0, blocks[0] - REACH), min(BLOCKS - 1, blocks[-1] + REACH)
                mine.append((j, low, high, base))
                base += high - low + 1
        runs.append(mine)
    return runs


RUNS = chip_runs()
CHIP_AT = [[CHIP_X[4 * side : 4 * side + 4].index(x) + 4 * side for x in range(4)] for side in range(2)]


def pick(index, values):
    result = jnp.int32(values[0])
    for place, value in enumerate(values[1:], 1):
        if value != values[0]:
            result = jnp.where(index == place, jnp.int32(value), result)
    return result


def run_code(k, j):
    for head, low, high, base in RUNS[k]:
        if head == j:
            return (low * 64 + high) * 64 + base
    return (63 * 64) * 64


def coordinates():
    block = lax.axis_index("blk")
    part = lax.axis_index("head")
    x, y_hi, core = block // 4, (block // 2) % 2, block % 2
    y_lo, z = part // 4, part % 4
    return block, x, y_hi, y_lo, 2 * y_hi + y_lo, z, core


def device(x, y, z, core):
    return (4 * x + 2 * (y // 2) + core, 4 * (y % 2) + z)


def my_chip(x, y):
    return pick(4 * (y % 2) + x, CHIP_AT[0] + CHIP_AT[1])


def frequency_rows():
    tables = np.zeros((3, 128), np.float32)
    start = 0
    for axis_id, count, span in ((0, 22, 44), (1, 21, 42), (2, 21, 42)):
        for column in range(count):
            rate = 1.0 / 10000.0 ** (2.0 * column / span)
            tables[axis_id, 2 * (start + column)] = rate
            tables[axis_id, 2 * (start + column) + 1] = rate
        start += count
    return tables


def swap_table():
    table = np.zeros((128, 128), np.float32)
    for pair in range(64):
        table[2 * pair + 1, 2 * pair] = -1.0
        table[2 * pair, 2 * pair + 1] = 1.0
    return table


def rotate_kernel(
    lists_ref, spots_ref, rates_ref, swap_ref, q_ref, k_ref, v_ref, dq_ref, dk_ref, dv_ref,
    kv_ref, qq_ref, table_ref, cos_ref, sin_ref,
):
    heads = kv_ref.shape[0]

    @pl.when(pl.program_id(0) == 0)
    def _():
        spots = spots_ref[...].astype(jnp.float32)
        angle = jnp.zeros((CHUNK, 128), jnp.float32)
        for axis_id in range(3):
            column = jnp.broadcast_to(spots[axis_id : axis_id + 1, :], (128, CHUNK)).T
            angle = angle + column * rates_ref[axis_id : axis_id + 1, :]
        cos_ref[...] = jnp.cos(angle)
        sin_ref[...] = jnp.sin(angle)
        _, x, _, _, y, _, core = coordinates()
        chip = my_chip(x, y)
        for i in range(3):
            job = 6 * chip + 2 * i + core
            j, block = job // 16, job % 16
            code = pick(3 * chip + j, [run_code(k, h) for k in range(8) for h in range(3)])
            low, base = code // 4096, code % 64
            last = jnp.int32(0)
            for s in range(5):
                entry = lists_ref[block, s]
                listed = entry >= 0
                last = jnp.where(listed, entry - low + base, last)
                table_ref[i, s] = last
                table_ref[3 + i, s] = listed.astype(jnp.int32)

    cosine, sine, swap = cos_ref[...], sin_ref[...], swap_ref[...]

    def turned(ref, lanes):
        part = ref[:, lanes]
        swapped = jnp.dot(part, swap, preferred_element_type=jnp.float32)
        return (part.astype(jnp.float32) * cosine + swapped * sine).astype(jnp.bfloat16)

    for head in range(heads):
        lanes = slice(128 * head, 128 * head + 128)
        kv_ref[head, :, 0:128] = turned(k_ref, lanes)
        kv_ref[head, :, 128:256] = turned(dk_ref, lanes)
        kv_ref[head, :, 256:384] = v_ref[:, lanes]
        kv_ref[head, :, 384:512] = dv_ref[:, lanes]
        qq_ref[head, :, 0:128] = turned(dq_ref, lanes)
        qq_ref[head, :, 128:256] = turned(q_ref, lanes)


def rotate_all(queries, keys, values, d_queries, d_keys, d_values, positions, key_lists):
    group = 4
    steps = 24 // group
    whole = pl.BlockSpec(memory_space=pltpu.VMEM)
    columns = pl.BlockSpec((CHUNK, 128 * group), lambda i: (0, i))
    return pl.pallas_call(
        rotate_kernel,
        name="rotate",
        grid=(steps,),
        out_shape=(
            jax.ShapeDtypeStruct((24, CHUNK, 512), jnp.bfloat16),
            jax.ShapeDtypeStruct((24, CHUNK, 256), jnp.bfloat16),
            jax.ShapeDtypeStruct((6, 5), jnp.int32),
        ),
        in_specs=[pl.BlockSpec(memory_space=pltpu.SMEM), whole, whole, whole] + [columns] * 6,
        out_specs=(
            pl.BlockSpec((group, CHUNK, 512), lambda i: (i, 0, 0)),
            pl.BlockSpec((group, CHUNK, 256), lambda i: (i, 0, 0)),
            pl.BlockSpec(memory_space=pltpu.SMEM),
        ),
        scratch_shapes=[pltpu.VMEM((CHUNK, 128), jnp.float32)] * 2,
        compiler_params=pltpu.CompilerParams(vmem_limit_bytes=32 * 2**20),
    )(
        key_lists, positions, jnp.asarray(frequency_rows()), jnp.asarray(swap_table(), jnp.bfloat16),
        queries, keys, values, d_queries, d_keys, d_values,
    )


def bring_kernel(
    pkv, pq, zkv, zq, ykv, yq, kv, qq,
    zs, zqs, ys, yqs, xs, xqs, fs, zr, zqr, yr, yqr, kr, qr, fr,
):
    block, x, y_hi, y_lo, y, z, core = coordinates()
    side = y % 2
    chip = my_chip(x, y)

    barrier = pltpu.get_barrier_semaphore()
    partners = (
        [device(x, y, (z + d) % 4, core) for d in (1, 2, 3)]
        + [device(x, (y + d) % 4, z, core) for d in (1, 2, 3)]
        + [device((x + d) % 4, y, z, core) for d in (1, 2, 3)]
        + [device(x, y, z, 1 - core)]
    )
    for partner in partners:
        pl.semaphore_signal(barrier, inc=1, device_id=partner, device_id_type=MESH)
    pl.semaphore_wait(barrier, len(partners))

    sent = []

    def send(where, here, source, target, send_sem, recv_sem, to):
        if here is not False:

            @pl.when(jnp.logical_and(where, here))
            def _():
                pltpu.make_async_copy(source, target, recv_sem).start()

        if here is not True:
            away = where if here is False else jnp.logical_and(where, jnp.logical_not(here))
            remote = pltpu.make_async_remote_copy(
                src_ref=source, dst_ref=target, send_sem=send_sem, recv_sem=recv_sem, device_id=to, device_id_type=MESH
            )

            @pl.when(away)
            def _():
                remote.start()

            sent.append((away, remote))

    def arrived(where, target, recv_sem):
        @pl.when(where)
        def _():
            pltpu.make_async_copy(target, target, recv_sem).wait()

    always = block >= 0
    rows_z = pl.ds(pl.multiple_of(z * CHUNK, CHUNK), CHUNK)
    for hh in ORDER:
        for d in (2, 1, 3, 0):
            to = (z + d) % 4
            head = 6 * to + hh
            place = device(x, y, to, core)
            send(always, d == 0, pkv.at[head], zkv.at[hh, rows_z], zs.at[hh, d], zr.at[hh], place)
            send(always, d == 0, pq.at[head], zq.at[hh, rows_z], zqs.at[hh, d], zqr.at[hh], place)

    rows_y = pl.ds(pl.multiple_of(y_lo * 512, 512), 512)

    def step_y(hh):
        g, j = hh // 3, hh % 3
        full = 1 if j == 1 else 0
        arrived(always, zkv.at[hh], zr.at[hh])
        for s in (0, 1):
            if (j, s) in ((0, 1), (2, 0)):
                continue
            where = always if j != 1 else (block <= 10 if s == 0 else block >= 5)
            to = 2 * g + s
            send(
                where, y == to, zkv.at[hh], ykv.at[full, y_hi, rows_y], ys.at[hh, s], yr.at[full, y_hi, y_lo],
                device(x, to, z, core),
            )
        arrived(always, zq.at[hh], zqr.at[hh])
        to = 2 * g + (16 * j + block) // 24
        send(
            always, y == to, zq.at[hh], yq.at[full, y_hi, rows_y], yqs.at[hh], yqr.at[full, y_hi],
            device(x, to, z, core),
        )

    def step_x(full):
        j = 1 if full else 2 * side
        for t in (0, 1):
            here = 4 * x + 2 * t + core
            came = always if full == 0 else jnp.logical_or(
                jnp.logical_and(side == 0, here <= 10), jnp.logical_and(side == 1, here >= 5)
            )
            for half in (0, 1):
                rows = pl.ds(512 * half, 512)
                arrived(came, ykv.at[full, t, rows], yr.at[full, t, half])
                for d in (2, 1, 3, 0):
                    to = (x + d) % 4
                    code = pick(
                        4 * side + to,
                        [run_code(CHIP_AT[s][xx], 1 if full else 2 * s) for s in range(2) for xx in range(4)],
                    )
                    low, high, base = code // 4096, (code // 64) % 64, code % 64
                    wanted = jnp.logical_and(here >= low, here <= high)
                    slot = jnp.where(wanted, here - low + base, 0)
                    send(
                        wanted, d == 0, ykv.at[full, t, rows], kv.at[slot, rows], xs.at[full, t, half, d], kr.at[slot],
                        device(to, y, z, core),
                    )
            job = 16 * j + here
            owned = job // 24 == side
            arrived(owned, yq.at[full, t], yqr.at[full, t])
            owner = job // 6
            to = pick(owner, CHIP_X)
            place = (job % 6) // 2
            send(
                owned, x == to, yq.at[full, t], qq.at[place], xqs.at[full, t], qr.at[place],
                device(to, y, z, core),
            )

    for hh in ORDER[:4]:
        step_y(hh)
    step_x(0)
    for hh in ORDER[4:]:
        step_y(hh)
    step_x(1)

    first = pick(chip, [RUNS[k][0][1] for k in range(8)])
    count = pick(chip, [sum(r[2] - r[1] + 1 for r in RUNS[k]) for k in range(8)])
    second = pick(chip, [RUNS[k][1][3] if len(RUNS[k]) > 1 else 63 for k in range(8)])
    second_low = pick(chip, [RUNS[k][1][1] if len(RUNS[k]) > 1 else 0 for k in range(8)])

    def slot_here(s):
        held = jnp.where(s < second, first + s, second_low + s - second)
        return s < count, held % 2 == core

    for s in range(SLOTS):
        used, mine = slot_here(s)
        direct = jnp.logical_and(used, mine)
        arrived(direct, kv.at[s], kr.at[s])
        send(direct, False, kv.at[s], kv.at[s], fs.at[s], fr.at[s], device(x, y, z, 1 - core))
    for s in range(SLOTS):
        used, mine = slot_here(s)
        arrived(jnp.logical_and(used, jnp.logical_not(mine)), kv.at[s], fr.at[s])
    for i in range(3):
        arrived(always, qq.at[i], qr.at[i])
    for away, remote in sent:

        @pl.when(away)
        def _():
            remote.wait_send()


def bring(pkv, pq):
    anywhere = pl.BlockSpec(memory_space=pl.ANY)
    dma = pltpu.SemaphoreType.DMA
    shapes = [
        (6, 512, 512), (6, 512, 256), (2, 2, QB, 512), (2, 2, QB, 256), (SLOTS, QB, 512), (3, QB, 256),
    ]
    sems = [
        (6, 4), (6, 4), (6, 2), (6,), (2, 2, 2, 4), (2, 2), (SLOTS,),
        (6,), (6,), (2, 2, 2), (2, 2), (SLOTS,), (3,), (SLOTS,),
    ]
    return pl.pallas_call(
        bring_kernel,
        name="bring",
        out_shape=tuple(jax.ShapeDtypeStruct(shape, jnp.bfloat16) for shape in shapes),
        in_specs=[anywhere] * 2,
        out_specs=(anywhere,) * len(shapes),
        scratch_shapes=[dma(shape) for shape in sems],
        compiler_params=pltpu.CompilerParams(collective_id=0, has_side_effects=True),
    )(pkv, pq)[4:]


def attend_kernel(table_ref, q_ref, kv_ref, out_ref, d_out_ref, top_ref, total_ref, light_ref, tilt_ref, rows=256):
    i, s = pl.program_id(0), pl.program_id(1)
    factor = SCALE * LOG2E

    @pl.when(s == 0)
    def _():
        top_ref[...] = jnp.full_like(top_ref, -jnp.inf)
        total_ref[...] = jnp.zeros_like(total_ref)
        light_ref[...] = jnp.zeros_like(light_ref)
        tilt_ref[...] = jnp.zeros_like(tilt_ref)

    @pl.when(table_ref[3 + i, s] == 1)
    def _():
        both_keys = kv_ref[0, :, 0:256]
        keys = kv_ref[0, :, 0:128]
        both_values = kv_ref[0, :, 256:512]
        ones = jnp.ones((QB, 128), jnp.bfloat16)
        values = jnp.concatenate([kv_ref[0, :, 256:384], ones], axis=1)
        across = (((1,), (1,)), ((), ()))

        for part in range(QB // rows):
            at = pl.ds(part * rows, rows)
            score = lax.dot_general(q_ref[0, at, 128:256], keys, across, preferred_element_type=jnp.float32)
            d_score = lax.dot_general(q_ref[0, at, :], both_keys, across, preferred_element_type=jnp.float32)
            old = top_ref[at, :]
            new = jnp.maximum(old, jnp.max(score, axis=1, keepdims=True))
            top_ref[at, :] = new
            fade = jnp.exp2((old - new) * factor)
            weight = jnp.exp2((score - new[:, 0:1]) * factor)
            tilted = weight * d_score
            partial = weight[:, 0:128]
            for c in range(1, QB // 128):
                partial = partial + weight[:, 128 * c : 128 * c + 128]
            total_ref[at, :] = total_ref[at, :] * fade + partial
            fade2 = jnp.concatenate([fade, fade], axis=1)
            light_ref[at, :] = light_ref[at, :] * fade2 + jnp.dot(
                weight.astype(jnp.bfloat16), both_values, preferred_element_type=jnp.float32
            )
            tilt_ref[at, :] = tilt_ref[at, :] * fade2 + jnp.dot(
                tilted.astype(jnp.bfloat16), values, preferred_element_type=jnp.float32
            )

    @pl.when(s == pl.num_programs(1) - 1)
    def _():
        inverse = 1.0 / jnp.sum(total_ref[...], axis=1, keepdims=True)
        out = light_ref[:, 0:128] * inverse
        moved = light_ref[:, 128:256] + SCALE * tilt_ref[:, 0:128]
        slope = SCALE * tilt_ref[:, 128:256]
        out_ref[0] = out.astype(jnp.bfloat16)
        d_out_ref[0] = (moved * inverse - slope * inverse * out).astype(jnp.bfloat16)


def attend(table, qq, kv):
    out = pl.BlockSpec((1, QB, 128), lambda i, s, table: (i, 0, 0))
    return pl.pallas_call(
        attend_kernel,
        name="attend",
        grid_spec=pltpu.PrefetchScalarGridSpec(
            num_scalar_prefetch=1,
            grid=(3, 5),
            in_specs=[
                pl.BlockSpec((1, QB, 256), lambda i, s, table: (i, 0, 0)),
                pl.BlockSpec((1, QB, 512), lambda i, s, table: (table[i, s], 0, 0)),
            ],
            out_specs=(out, out),
            scratch_shapes=[
                pltpu.VMEM((QB, 128), jnp.float32),
                pltpu.VMEM((QB, 128), jnp.float32),
                pltpu.VMEM((QB, 256), jnp.float32),
                pltpu.VMEM((QB, 256), jnp.float32),
            ],
        ),
        out_shape=(jax.ShapeDtypeStruct((3, QB, 128), jnp.bfloat16),) * 2,
        compiler_params=pltpu.CompilerParams(vmem_limit_bytes=48 * 2**20),
    )(table, qq, kv)


def return_kernel(out, d_out, attended, d_attended, ss, dss, rs, drs):
    block, x, y_hi, y_lo, y, z, core = coordinates()
    chip = my_chip(x, y)
    barrier = pltpu.get_barrier_semaphore()
    own = jnp.int32(0)
    for z_from in range(4):
        for g in range(2):
            for j in range(3):
                owner = (16 * j + block) // 6
                x_from, y_from = pick(owner, CHIP_X), 2 * g + owner // 4
                me = jnp.logical_and(jnp.logical_and(x_from == x, y_from == y), z == z_from)
                own = own + me.astype(jnp.int32)

                @pl.when(jnp.logical_not(me))
                def _():
                    pl.semaphore_signal(
                        barrier, inc=1, device_id=device(x_from, y_from, z_from, core), device_id_type=MESH
                    )

    pl.semaphore_wait(barrier, 24 - own)

    sent = []
    for i in range(3):
        job = 6 * chip + 2 * i + core
        j, b = job // 16, job % 16
        lanes = pl.ds(pl.multiple_of((6 * z + 3 * (y // 2) + j) * 128, 128), 128)
        for d in range(8):
            p = (d + 4 * y_lo + z) % 8
            rows = pl.ds(pl.multiple_of(p * CHUNK, CHUNK), CHUNK)
            me = jnp.logical_and(b == block, p == 4 * y_lo + z)
            for source, target, sends, recv in ((out, attended, ss, rs), (d_out, d_attended, dss, drs)):
                from_ref, to_ref = source.at[i, rows], target.at[:, lanes]
                remote = pltpu.make_async_remote_copy(
                    src_ref=from_ref, dst_ref=to_ref, send_sem=sends.at[i, d], recv_sem=recv,
                    device_id=(b, p), device_id_type=MESH,
                )

                @pl.when(me)
                def _():
                    pltpu.make_async_copy(from_ref, to_ref, recv).start()

                @pl.when(jnp.logical_not(me))
                def _():
                    remote.start()

                sent.append((me, remote))
    pltpu.make_async_copy(attended, attended, rs).wait()
    pltpu.make_async_copy(d_attended, d_attended, drs).wait()
    for me, remote in sent:

        @pl.when(jnp.logical_not(me))
        def _():
            remote.wait_send()


def bring_back(out, d_out):
    anywhere = pl.BlockSpec(memory_space=pl.ANY)
    dma = pltpu.SemaphoreType.DMA
    return pl.pallas_call(
        return_kernel,
        name="bring_back",
        out_shape=(jax.ShapeDtypeStruct((CHUNK, 3072), jnp.bfloat16),) * 2,
        in_specs=[anywhere] * 2,
        out_specs=(anywhere,) * 2,
        scratch_shapes=[dma((3, 8)), dma((3, 8)), dma, dma],
        compiler_params=pltpu.CompilerParams(collective_id=1, has_side_effects=True),
    )(out, d_out)


def on_device(queries, keys, values, d_queries, d_keys, d_values, positions, key_lists):
    pkv, pq, table = rotate_all(queries, keys, values, d_queries, d_keys, d_values, positions, key_lists)
    kv, qq = bring(pkv, pq)
    out, d_out = attend(table, qq, kv)
    return bring_back(out, d_out)


def solution(mesh):
    tokens = P(("blk", "head"), None)
    return jax.shard_map(
        on_device,
        mesh=mesh,
        in_specs=(tokens,) * 6 + (P(None, ("blk", "head")), P()),
        out_specs=(tokens, tokens),
        check_vma=False,
    )
```

```python
import functools

import jax
import jax.numpy as jnp
import numpy as np
from jax import lax
from jax.experimental import pallas as pl
from jax.experimental.pallas import tpu as pltpu
from jax.sharding import PartitionSpec as P

MESH = pl.DeviceIdType.MESH
REACH = 3
BLOCKS = 16
CHUNK = 128
QB = 1024
SCALE = 128 ** (-0.5)
LOG2E = 1.4426950408889634
CHIP_X = (0, 2, 3, 1, 2, 0, 1, 3)
SLOTS = 12


def chip_runs():
    runs = []
    for k in range(8):
        mine, base = [], 0
        for j in range(3):
            blocks = [job % 16 for job in range(6 * k, 6 * k + 6) if job // 16 == j]
            if blocks:
                low, high = max(0, blocks[0] - REACH), min(BLOCKS - 1, blocks[-1] + REACH)
                mine.append((j, low, high, base))
                base += high - low + 1
        runs.append(mine)
    return runs


RUNS = chip_runs()
CHIP_AT = [[CHIP_X[4 * side : 4 * side + 4].index(x) + 4 * side for x in range(4)] for side in range(2)]


def pick(index, values):
    result = jnp.int32(values[0])
    for place, value in enumerate(values[1:], 1):
        if value != values[0]:
            result = jnp.where(index == place, jnp.int32(value), result)
    return result


def run_code(k, j):
    for head, low, high, base in RUNS[k]:
        if head == j:
            return (low * 64 + high) * 64 + base
    return (63 * 64) * 64


def coordinates():
    block = lax.axis_index("blk")
    part = lax.axis_index("head")
    x, y_hi, core = block // 4, (block // 2) % 2, block % 2
    y_lo, z = part // 4, part % 4
    return block, x, y_hi, y_lo, 2 * y_hi + y_lo, z, core


def device(x, y, z, core):
    return (4 * x + 2 * (y // 2) + core, 4 * (y % 2) + z)


def my_chip(x, y):
    return pick(4 * (y % 2) + x, CHIP_AT[0] + CHIP_AT[1])


def frequency_rows():
    tables = np.zeros((3, 128), np.float32)
    start = 0
    for axis_id, count, span in ((0, 22, 44), (1, 21, 42), (2, 21, 42)):
        for column in range(count):
            rate = 1.0 / 10000.0 ** (2.0 * column / span)
            tables[axis_id, 2 * (start + column)] = rate
            tables[axis_id, 2 * (start + column) + 1] = rate
        start += count
    return tables


def swap_table():
    table = np.zeros((128, 128), np.float32)
    for pair in range(64):
        table[2 * pair + 1, 2 * pair] = -1.0
        table[2 * pair, 2 * pair + 1] = 1.0
    return table


def rotate_kernel(
    lists_ref, spots_ref, rates_ref, swap_ref, q_ref, k_ref, v_ref, dq_ref, dk_ref, dv_ref,
    kv_ref, qq_ref, table_ref, cos_ref, sin_ref,
):
    heads = kv_ref.shape[0]

    @pl.when(pl.program_id(0) == 0)
    def _():
        spots = spots_ref[...].astype(jnp.float32)
        angle = jnp.zeros((CHUNK, 128), jnp.float32)
        for axis_id in range(3):
            column = jnp.broadcast_to(spots[axis_id : axis_id + 1, :], (128, CHUNK)).T
            angle = angle + column * rates_ref[axis_id : axis_id + 1, :]
        cos_ref[...] = jnp.cos(angle)
        sin_ref[...] = jnp.sin(angle)
        _, x, _, _, y, _, core = coordinates()
        chip = my_chip(x, y)
        for i in range(3):
            job = 6 * chip + 2 * i + core
            j, block = job // 16, job % 16
            code = pick(3 * chip + j, [run_code(k, h) for k in range(8) for h in range(3)])
            low, base = code // 4096, code % 64
            last = jnp.int32(0)
            for s in range(5):
                entry = lists_ref[block, s]
                listed = entry >= 0
                last = jnp.where(listed, entry - low + base, last)
                table_ref[i, s] = last
                table_ref[3 + i, s] = listed.astype(jnp.int32)

    cosine, sine, swap = cos_ref[...], sin_ref[...], swap_ref[...]

    def turned(ref, lanes):
        part = ref[:, lanes]
        swapped = jnp.dot(part, swap, preferred_element_type=jnp.float32)
        return (part.astype(jnp.float32) * cosine + swapped * sine).astype(jnp.bfloat16)

    for head in range(heads):
        lanes = slice(128 * head, 128 * head + 128)
        kv_ref[head, :, 0:128] = turned(k_ref, lanes)
        kv_ref[head, :, 128:256] = turned(dk_ref, lanes)
        kv_ref[head, :, 256:384] = v_ref[:, lanes]
        kv_ref[head, :, 384:512] = dv_ref[:, lanes]
        qq_ref[head, :, 0:128] = turned(dq_ref, lanes)
        qq_ref[head, :, 128:256] = turned(q_ref, lanes)


def rotate_all(queries, keys, values, d_queries, d_keys, d_values, positions, key_lists):
    group = 4
    steps = 24 // group
    whole = pl.BlockSpec(memory_space=pltpu.VMEM)
    columns = pl.BlockSpec((CHUNK, 128 * group), lambda i: (0, i))
    return pl.pallas_call(
        rotate_kernel,
        name="rotate",
        grid=(steps,),
        out_shape=(
            jax.ShapeDtypeStruct((24, CHUNK, 512), jnp.bfloat16),
            jax.ShapeDtypeStruct((24, CHUNK, 256), jnp.bfloat16),
            jax.ShapeDtypeStruct((6, 5), jnp.int32),
        ),
        in_specs=[pl.BlockSpec(memory_space=pltpu.SMEM), whole, whole, whole] + [columns] * 6,
        out_specs=(
            pl.BlockSpec((group, CHUNK, 512), lambda i: (i, 0, 0)),
            pl.BlockSpec((group, CHUNK, 256), lambda i: (i, 0, 0)),
            pl.BlockSpec(memory_space=pltpu.SMEM),
        ),
        scratch_shapes=[pltpu.VMEM((CHUNK, 128), jnp.float32)] * 2,
        compiler_params=pltpu.CompilerParams(vmem_limit_bytes=32 * 2**20),
    )(
        key_lists, positions, jnp.asarray(frequency_rows()), jnp.asarray(swap_table(), jnp.bfloat16),
        queries, keys, values, d_queries, d_keys, d_values,
    )


KV_WAIT, KV_ROWS = (SLOTS + 4) * QB, (SLOTS + 7) * QB
Q_PASS, Q_WAIT, Q_ROWS = 3 * QB, 7 * QB, 10 * QB
CODES = [run_code(CHIP_AT[side][x], j) for j in range(3) for side in range(2) for x in range(4)]


def window(x, side, j):
    code = pick(8 * j + 4 * side + x, CODES)
    return code // 4096, (code // 64) % 64, code % 64


def wants(side, block):
    return jnp.where(side == 0, block <= 10, block >= 5)


def kv_place(x, side, j, block):
    low, high, base = window(x, side, j)
    inside = jnp.logical_and(block >= low, block <= high)
    full = 1 if isinstance(j, int) and j == 1 else jnp.where(j == 1, 1, 0)
    return jnp.where(inside, block - low + base, SLOTS + 2 * full + (block // 2) % 2)


def q_place(x, j, block):
    job = 16 * j + block
    full = 1 if isinstance(j, int) and j == 1 else jnp.where(j == 1, 1, 0)
    passing = Q_PASS + (2 * full + (block // 2) % 2) * QB
    return jnp.where(pick(job // 6, CHIP_X) == x, (job % 6) // 2 * QB, passing)


def at_rows(ref, first, count, step):
    return ref.at[pl.ds(pl.multiple_of(first, step), count)]


def bring_kernel(
    pkv, pq, kv, qq,
    zs, zqs, ys, yqs, xs, xqs, fs, zr, zqr, yr, yqr, kr, qr, fr,
):
    block, x, y_hi, y_lo, y, z, core = coordinates()
    side = y % 2
    chip = my_chip(x, y)
    always = block >= 0
    no, both = jnp.logical_not, jnp.logical_and

    barrier = pltpu.get_barrier_semaphore()
    partners = (
        [device(x, y, (z + d) % 4, core) for d in (1, 2, 3)]
        + [device(x, (y + d) % 4, z, core) for d in (1, 2, 3)]
        + [device((x + d) % 4, y, z, core) for d in (1, 2, 3)]
        + [device(x, y, z, 1 - core)]
    )
    for partner in partners:
        pl.semaphore_signal(barrier, inc=1, device_id=partner, device_id_type=MESH)
    pl.semaphore_wait(barrier, len(partners))

    sent = []

    def send(where, source, target, send_sem, recv_sem, to):
        remote = pltpu.make_async_remote_copy(
            src_ref=source, dst_ref=target, send_sem=send_sem, recv_sem=recv_sem, device_id=to, device_id_type=MESH
        )

        @pl.when(where)
        def _():
            remote.start()

        sent.append((where, remote))

    def arrived(where, target, recv_sem):
        @pl.when(where)
        def _():
            pltpu.make_async_copy(target, target, recv_sem).wait()


    def kv_after_z(hh, start, size):
        g, j = hh // 3, hh % 3
        stays = both(y_hi == g, side == j // 2 if j != 1 else wants(side, block))
        in_place = kv_place(x, side, j, block) * QB + start + y_lo * (size // 2)
        return jnp.where(stays, in_place, KV_WAIT + hh * 512 + start // 2)

    def q_after_z(hh):
        g, j = hh // 3, hh % 3
        stays = both(y_hi == g, side == (16 * j + block) // 24)
        return stays, jnp.where(stays, q_place(x, j, block) + y_lo * 512, Q_WAIT + hh * 512)

    def z_kv(mid, part, start, size):
        for hh in (1, 4) if mid else (0, 5, 2, 3):
            count = size // 8
            to_rows = at_rows(kv, kv_after_z(hh, start, size) + z * count, count, STEP // 8)
            for d in (2, 1, 3, 0):
                to = (z + d) % 4
                from_rows = pkv.at[6 * to + hh, pl.ds(start // 8, count)]
                if d:
                    send(always, from_rows, to_rows, zs.at[hh, part, d], zr.at[hh, part], device(x, y, to, core))
                else:
                    pltpu.make_async_copy(from_rows, to_rows, zr.at[hh, part]).start()

    def z_q(hh):
        _, row = q_after_z(hh)
        to_rows = at_rows(qq, row + z * CHUNK, CHUNK, CHUNK)
        for d in (2, 1, 3, 0):
            to = (z + d) % 4
            if d:
                send(always, pq.at[6 * to + hh], to_rows, zqs.at[hh, d], zqr.at[hh], device(x, y, to, core))
            else:
                pltpu.make_async_copy(pq.at[6 * to + hh], to_rows, zqr.at[hh]).start()

    def y_kv(mid, part, start, size):
        count = size // 2
        for hh in (1, 4) if mid else (0, 5, 2, 3):
            g, j = hh // 3, hh % 3
            source = at_rows(kv, kv_after_z(hh, start, size), count, STEP // 2)
            arrived(always, source, zr.at[hh, part])
            for s in (0, 1) if mid else (j // 2,):
                where = wants(jnp.int32(s), block) if mid else always
                to = 2 * g + s
                row = kv_place(x, s, j, block) * QB + start + y_lo * count
                send(
                    both(where, y != to), source, at_rows(kv, row, count, STEP // 2),
                    ys.at[hh, s, part], yr.at[mid, y_hi, y_lo, part], device(x, to, z, core),
                )

    def y_q(hh):
        g, j = hh // 3, hh % 3
        stays, row = q_after_z(hh)
        source = at_rows(qq, row, 512, 512)
        arrived(always, source, zqr.at[hh])
        send(
            no(stays), source, at_rows(qq, q_place(x, j, block) + y_lo * 512, 512, 512),
            yqs.at[hh], yqr.at[j % 2, y_hi, y_lo], device(x, 2 * g + (16 * j + block) // 24, z, core),
        )

    def x_kv(mid, part, start, size):
        j = 1 if mid else 2 * side
        for t in (0, 1):
            here = 4 * x + 2 * t + core
            came = wants(side, here) if mid else always
            place = kv_place(x, side, j, here)
            row = place * QB + start
            for half in (0, 1):
                own = both(t == y_hi, half == y_lo)
                rows = at_rows(kv, row + half * (size // 2), size // 2, STEP // 2)
                arrived(both(came, no(own)), rows, yr.at[mid, t, half, part])
            source = at_rows(kv, row, size, STEP)
            for d in (2, 1, 3):
                to = (x + d) % 4
                low, high, base = window(to, side, j)
                wanted = both(here >= low, here <= high)
                slot = jnp.where(wanted, here - low + base, 0)
                send(
                    wanted, source, at_rows(kv, slot * QB + start, size, STEP),
                    xs.at[mid, t, d, part], kr.at[slot, part], device(to, y, z, core),
                )
            kept = both(came, place < SLOTS)
            slot = jnp.where(kept, place, 0)
            rows = at_rows(kv, slot * QB + start, size, STEP)
            send(kept, rows, rows, fs.at[mid, t, 0, part], fr.at[slot, part], device(x, y, z, 1 - core))

    def x_q(full_or_mid):
        mid = full_or_mid
        j = 1 if mid else 2 * side
        for t in (0, 1):
            job = 16 * j + 4 * x + 2 * t + core
            owned = job // 24 == side
            row = q_place(x, j, 4 * x + 2 * t + core)
            for half in (0, 1):
                own = both(t == y_hi, half == y_lo)
                arrived(both(owned, no(own)), at_rows(qq, row + half * 512, 512, 512), yqr.at[mid, t, half])
            to = pick(job // 6, CHIP_X)
            slot = (job % 6) // 2
            send(
                both(owned, to != x), at_rows(qq, row, QB, QB), at_rows(qq, slot * QB, QB, QB),
                xqs.at[mid, t], qr.at[slot], device(to, y, z, core),
            )

    def wanted_here(mid, t, d, other):
        low, high, base = window(x, side, 1 if mid else 2 * side)
        from_block = 4 * ((x + d) % 4) + 2 * t + (1 - core if other else core)
        wanted = both(from_block >= low, from_block <= high)
        return wanted, jnp.where(wanted, from_block - low + base, 0)

    def to_other_core(mid, part, start, size):
        for d in (1, 3, 2):
            for t in (0, 1):
                wanted, slot = wanted_here(mid, t, d, False)
                rows = at_rows(kv, slot * QB + start, size, STEP)
                arrived(wanted, rows, kr.at[slot, part])
                send(wanted, rows, rows, fs.at[mid, t, d, part], fr.at[slot, part], device(x, y, z, 1 - core))

    stages = {"z": z_kv, "y": y_kv, "x": x_kv, "c": to_other_core}
    stages_q = {"z": z_q, "y": y_q, "x": x_q}
    for name, item in SCHEDULE:
        if isinstance(item, tuple):
            for mid in (0, 1):
                stages[name](mid, *item)
        else:
            stages_q[name](item)

    for part, start, size in PARTS:
        for mid, t in ((0, 0), (0, 1), (1, 0), (1, 1)):
            for d in (0, 1, 3, 2):
                wanted, slot = wanted_here(mid, t, d, True)
                arrived(wanted, at_rows(kv, slot * QB + start, size, STEP), fr.at[slot, part])
    for i in range(3):
        b = (6 * chip + 2 * i + core) % 16
        arrived(b // 4 != x, at_rows(qq, i * QB, QB, QB), qr.at[i])
    for where, remote in sent:

        @pl.when(where)
        def _():
            remote.wait_send()


STEP = 128
SIZES = (128, 128, 256, 256, 256)
PARTS = [(part, sum(SIZES[:part]), size) for part, size in enumerate(SIZES)]
Q_ORDER = (0, 5, 2, 3, 1, 4)


def make_schedule(lead, lag_x, lag_c):
    steps = [("kv", part) for part in PARTS] + [("q", Q_ORDER[2 * i : 2 * i + 2]) for i in range(3)]
    schedule = []

    def add(stage, index):
        if 0 <= index < len(steps):
            kind, item = steps[index]
            if kind == "kv":
                schedule.append((stage, item))
            elif stage in "zy":
                schedule.extend((stage, hh) for hh in item)

    for step in range(lead):
        add("z", step)
    for step in range(len(steps) + max(lag_x, lag_c)):
        add("y", step)
        add("z", step + lead)
        add("x", step - lag_x)
        add("c", step - lag_c)
    return schedule + [("x", 0), ("x", 1)]


SCHEDULE = make_schedule(3, 1, 3)


def bring(pkv, pq):
    anywhere = pl.BlockSpec(memory_space=pl.ANY)
    dma = pltpu.SemaphoreType.DMA
    n = len(PARTS)
    sems = [
        (6, n, 4), (6, 4), (6, 2, n), (6,), (2, 2, 4, n), (2, 2), (2, 2, 4, n),
        (6, n), (6,), (2, 2, 2, n), (2, 2, 2), (SLOTS, n), (3,), (SLOTS, n),
    ]
    return pl.pallas_call(
        bring_kernel,
        name="bring",
        out_shape=(
            jax.ShapeDtypeStruct((KV_ROWS, 512), jnp.bfloat16), jax.ShapeDtypeStruct((Q_ROWS, 256), jnp.bfloat16),
        ),
        in_specs=[anywhere] * 2,
        out_specs=(anywhere,) * 2,
        scratch_shapes=[dma(shape) for shape in sems],
        compiler_params=pltpu.CompilerParams(collective_id=0, has_side_effects=True),
    )(pkv, pq)


def attend_kernel(table_ref, q_ref, kv_ref, out_ref, d_out_ref, top_ref, total_ref, light_ref, tilt_ref, rows=256):
    i, s = pl.program_id(0), pl.program_id(1)
    factor = SCALE * LOG2E

    @pl.when(s == 0)
    def _():
        top_ref[...] = jnp.full_like(top_ref, -jnp.inf)
        total_ref[...] = jnp.zeros_like(total_ref)
        light_ref[...] = jnp.zeros_like(light_ref)
        tilt_ref[...] = jnp.zeros_like(tilt_ref)

    @pl.when(table_ref[3 + i, s] == 1)
    def _():
        both_keys = kv_ref[:, 0:256]
        keys = kv_ref[:, 0:128]
        both_values = kv_ref[:, 256:512]
        ones = jnp.ones((QB, 128), jnp.bfloat16)
        values = jnp.concatenate([kv_ref[:, 256:384], ones], axis=1)
        across = (((1,), (1,)), ((), ()))

        for part in range(QB // rows):
            at = pl.ds(part * rows, rows)
            score = lax.dot_general(q_ref[at, 128:256], keys, across, preferred_element_type=jnp.float32)
            d_score = lax.dot_general(q_ref[at, :], both_keys, across, preferred_element_type=jnp.float32)
            old = top_ref[at, :]
            new = jnp.maximum(old, jnp.max(score, axis=1, keepdims=True))
            top_ref[at, :] = new
            fade = jnp.exp2((old - new) * factor)
            weight = jnp.exp2((score - new[:, 0:1]) * factor)
            tilted = weight * d_score
            partial = weight[:, 0:128]
            for c in range(1, QB // 128):
                partial = partial + weight[:, 128 * c : 128 * c + 128]
            total_ref[at, :] = total_ref[at, :] * fade + partial
            fade2 = jnp.concatenate([fade, fade], axis=1)
            light_ref[at, :] = light_ref[at, :] * fade2 + jnp.dot(
                weight.astype(jnp.bfloat16), both_values, preferred_element_type=jnp.float32
            )
            tilt_ref[at, :] = tilt_ref[at, :] * fade2 + jnp.dot(
                tilted.astype(jnp.bfloat16), values, preferred_element_type=jnp.float32
            )

    @pl.when(s == pl.num_programs(1) - 1)
    def _():
        inverse = 1.0 / jnp.sum(total_ref[...], axis=1, keepdims=True)
        out = light_ref[:, 0:128] * inverse
        moved = light_ref[:, 128:256] + SCALE * tilt_ref[:, 0:128]
        slope = SCALE * tilt_ref[:, 128:256]
        out_ref[0] = out.astype(jnp.bfloat16)
        d_out_ref[0] = (moved * inverse - slope * inverse * out).astype(jnp.bfloat16)


def attend(table, qq, kv):
    out = pl.BlockSpec((1, QB, 128), lambda i, s, table: (i, 0, 0))
    return pl.pallas_call(
        attend_kernel,
        name="attend",
        grid_spec=pltpu.PrefetchScalarGridSpec(
            num_scalar_prefetch=1,
            grid=(3, 5),
            in_specs=[
                pl.BlockSpec((QB, 256), lambda i, s, table: (i, 0)),
                pl.BlockSpec((QB, 512), lambda i, s, table: (table[i, s], 0)),
            ],
            out_specs=(out, out),
            scratch_shapes=[
                pltpu.VMEM((QB, 128), jnp.float32),
                pltpu.VMEM((QB, 128), jnp.float32),
                pltpu.VMEM((QB, 256), jnp.float32),
                pltpu.VMEM((QB, 256), jnp.float32),
            ],
        ),
        out_shape=(jax.ShapeDtypeStruct((3, QB, 128), jnp.bfloat16),) * 2,
        compiler_params=pltpu.CompilerParams(vmem_limit_bytes=48 * 2**20),
    )(table, qq, kv)


def return_kernel(out, d_out, attended, d_attended, ss, dss, rs, drs):
    block, x, y_hi, y_lo, y, z, core = coordinates()
    chip = my_chip(x, y)
    barrier = pltpu.get_barrier_semaphore()
    own = jnp.int32(0)
    for z_from in range(4):
        for g in range(2):
            for j in range(3):
                owner = (16 * j + block) // 6
                x_from, y_from = pick(owner, CHIP_X), 2 * g + owner // 4
                me = jnp.logical_and(jnp.logical_and(x_from == x, y_from == y), z == z_from)
                own = own + me.astype(jnp.int32)

                @pl.when(jnp.logical_not(me))
                def _():
                    pl.semaphore_signal(
                        barrier, inc=1, device_id=device(x_from, y_from, z_from, core), device_id_type=MESH
                    )

    pl.semaphore_wait(barrier, 24 - own)

    sent = []
    for i in range(3):
        job = 6 * chip + 2 * i + core
        j, b = job // 16, job % 16
        lanes = pl.ds(pl.multiple_of((6 * z + 3 * (y // 2) + j) * 128, 128), 128)
        for d in range(8):
            p = (d + 4 * y_lo + z) % 8
            rows = pl.ds(pl.multiple_of(p * CHUNK, CHUNK), CHUNK)
            me = jnp.logical_and(b == block, p == 4 * y_lo + z)
            for source, target, sends, recv in ((out, attended, ss, rs), (d_out, d_attended, dss, drs)):
                from_ref, to_ref = source.at[i, rows], target.at[:, lanes]
                remote = pltpu.make_async_remote_copy(
                    src_ref=from_ref, dst_ref=to_ref, send_sem=sends.at[i, d], recv_sem=recv,
                    device_id=(b, p), device_id_type=MESH,
                )

                @pl.when(me)
                def _():
                    pltpu.make_async_copy(from_ref, to_ref, recv).start()

                @pl.when(jnp.logical_not(me))
                def _():
                    remote.start()

                sent.append((me, remote))
    pltpu.make_async_copy(attended, attended, rs).wait()
    pltpu.make_async_copy(d_attended, d_attended, drs).wait()
    for me, remote in sent:

        @pl.when(jnp.logical_not(me))
        def _():
            remote.wait_send()


def bring_back(out, d_out):
    anywhere = pl.BlockSpec(memory_space=pl.ANY)
    dma = pltpu.SemaphoreType.DMA
    return pl.pallas_call(
        return_kernel,
        name="bring_back",
        out_shape=(jax.ShapeDtypeStruct((CHUNK, 3072), jnp.bfloat16),) * 2,
        in_specs=[anywhere] * 2,
        out_specs=(anywhere,) * 2,
        scratch_shapes=[dma((3, 8)), dma((3, 8)), dma, dma],
        compiler_params=pltpu.CompilerParams(collective_id=1, has_side_effects=True),
    )(out, d_out)


def on_device(queries, keys, values, d_queries, d_keys, d_values, positions, key_lists):
    pkv, pq, table = rotate_all(queries, keys, values, d_queries, d_keys, d_values, positions, key_lists)
    kv, qq = bring(pkv, pq)
    out, d_out = attend(table, qq, kv)
    return bring_back(out, d_out)


def solution(mesh):
    tokens = P(("blk", "head"), None)
    return jax.shard_map(
        on_device,
        mesh=mesh,
        in_specs=(tokens,) * 6 + (P(None, ("blk", "head")), P()),
        out_specs=(tokens, tokens),
        check_vma=False,
    )
```

```python
import functools

import jax
import jax.numpy as jnp
import numpy as np
from jax import lax
from jax.experimental import pallas as pl
from jax.experimental.pallas import tpu as pltpu
from jax.sharding import PartitionSpec as P

MESH = pl.DeviceIdType.MESH
REACH = 3
BLOCKS = 16
CHUNK = 128
QB = 1024
SCALE = 128 ** (-0.5)
LOG2E = 1.4426950408889634
CHIP_X = (0, 2, 3, 1, 2, 0, 1, 3)
SLOTS = 12


def chip_runs():
    runs = []
    for k in range(8):
        mine, base = [], 0
        for j in range(3):
            blocks = [job % 16 for job in range(6 * k, 6 * k + 6) if job // 16 == j]
            if blocks:
                low, high = max(0, blocks[0] - REACH), min(BLOCKS - 1, blocks[-1] + REACH)
                mine.append((j, low, high, base))
                base += high - low + 1
        runs.append(mine)
    return runs


RUNS = chip_runs()
CHIP_AT = [[CHIP_X[4 * side : 4 * side + 4].index(x) + 4 * side for x in range(4)] for side in range(2)]


def pick(index, values):
    result = jnp.int32(values[0])
    for place, value in enumerate(values[1:], 1):
        if value != values[0]:
            result = jnp.where(index == place, jnp.int32(value), result)
    return result


def run_code(k, j):
    for head, low, high, base in RUNS[k]:
        if head == j:
            return (low * 64 + high) * 64 + base
    return (63 * 64) * 64


def coordinates():
    block = lax.axis_index("blk")
    part = lax.axis_index("head")
    x, y_hi, core = block // 4, (block // 2) % 2, block % 2
    y_lo, z = part // 4, part % 4
    return block, x, y_hi, y_lo, 2 * y_hi + y_lo, z, core


def device(x, y, z, core):
    return (4 * x + 2 * (y // 2) + core, 4 * (y % 2) + z)


def my_chip(x, y):
    return pick(4 * (y % 2) + x, CHIP_AT[0] + CHIP_AT[1])


def frequency_rows():
    tables = np.zeros((3, 128), np.float32)
    start = 0
    for axis_id, count, span in ((0, 22, 44), (1, 21, 42), (2, 21, 42)):
        for column in range(count):
            rate = 1.0 / 10000.0 ** (2.0 * column / span)
            tables[axis_id, 2 * (start + column)] = rate
            tables[axis_id, 2 * (start + column) + 1] = rate
        start += count
    return tables


def swap_table():
    table = np.zeros((128, 128), np.float32)
    for pair in range(64):
        table[2 * pair + 1, 2 * pair] = -1.0
        table[2 * pair, 2 * pair + 1] = 1.0
    return table


def rotate_kernel(
    lists_ref, spots_ref, rates_ref, swap_ref, q_ref, k_ref, v_ref, dq_ref, dk_ref, dv_ref,
    kv_ref, qq_ref, table_ref, cos_ref, sin_ref,
):
    heads = kv_ref.shape[0]

    @pl.when(pl.program_id(0) == 0)
    def _():
        spots = spots_ref[...].astype(jnp.float32)
        angle = jnp.zeros((CHUNK, 128), jnp.float32)
        for axis_id in range(3):
            column = jnp.broadcast_to(spots[axis_id : axis_id + 1, :], (128, CHUNK)).T
            angle = angle + column * rates_ref[axis_id : axis_id + 1, :]
        cos_ref[...] = jnp.cos(angle)
        sin_ref[...] = jnp.sin(angle)
        _, x, _, _, y, _, core = coordinates()
        chip = my_chip(x, y)
        for i in range(3):
            job = 6 * chip + 2 * i + core
            j, block = job // 16, job % 16
            code = pick(3 * chip + j, [run_code(k, h) for k in range(8) for h in range(3)])
            low, base = code // 4096, code % 64
            last = jnp.int32(0)
            for s in range(5):
                entry = lists_ref[block, s]
                listed = entry >= 0
                last = jnp.where(listed, entry - low + base, last)
                table_ref[i, s] = last
                table_ref[3 + i, s] = listed.astype(jnp.int32)

    cosine, sine, swap = cos_ref[...], sin_ref[...], swap_ref[...]

    def turned(ref, lanes):
        part = ref[:, lanes]
        swapped = jnp.dot(part, swap, preferred_element_type=jnp.float32)
        return (part.astype(jnp.float32) * cosine + swapped * sine).astype(jnp.bfloat16)

    for head in range(heads):
        lanes = slice(128 * head, 128 * head + 128)
        kv_ref[head, :, 0:128] = turned(k_ref, lanes)
        kv_ref[head, :, 128:256] = turned(dk_ref, lanes)
        kv_ref[head, :, 256:384] = v_ref[:, lanes]
        kv_ref[head, :, 384:512] = dv_ref[:, lanes]
        qq_ref[head, :, 0:128] = turned(dq_ref, lanes)
        qq_ref[head, :, 128:256] = turned(q_ref, lanes)


def rotate_all(queries, keys, values, d_queries, d_keys, d_values, positions, key_lists):
    group = 4
    steps = 24 // group
    whole = pl.BlockSpec(memory_space=pltpu.VMEM)
    columns = pl.BlockSpec((CHUNK, 128 * group), lambda i: (0, i))
    return pl.pallas_call(
        rotate_kernel,
        name="rotate",
        grid=(steps,),
        out_shape=(
            jax.ShapeDtypeStruct((24, CHUNK, 512), jnp.bfloat16),
            jax.ShapeDtypeStruct((24, CHUNK, 256), jnp.bfloat16),
            jax.ShapeDtypeStruct((6, 5), jnp.int32),
        ),
        in_specs=[pl.BlockSpec(memory_space=pltpu.SMEM), whole, whole, whole] + [columns] * 6,
        out_specs=(
            pl.BlockSpec((group, CHUNK, 512), lambda i: (i, 0, 0)),
            pl.BlockSpec((group, CHUNK, 256), lambda i: (i, 0, 0)),
            pl.BlockSpec(memory_space=pltpu.SMEM),
        ),
        scratch_shapes=[pltpu.VMEM((CHUNK, 128), jnp.float32)] * 2,
        compiler_params=pltpu.CompilerParams(vmem_limit_bytes=32 * 2**20),
    )(
        key_lists, positions, jnp.asarray(frequency_rows()), jnp.asarray(swap_table(), jnp.bfloat16),
        queries, keys, values, d_queries, d_keys, d_values,
    )


GROUP = 256
KV_WAIT = (SLOTS + 4) * GROUP
Q_PASS, Q_WAIT, Q_ROWS = 3 * QB, 7 * QB, 10 * QB
CODES = [run_code(CHIP_AT[side][x], j) for j in range(3) for side in range(2) for x in range(4)]


def window(x, side, j):
    code = pick(8 * j + 4 * side + x, CODES)
    return code // 4096, (code // 64) % 64, code % 64


def wants(side, block):
    return jnp.where(side == 0, block <= 10, block >= 5)


def kv_place(x, side, j, block):
    low, high, base = window(x, side, j)
    inside = jnp.logical_and(block >= low, block <= high)
    full = 1 if isinstance(j, int) and j == 1 else jnp.where(j == 1, 1, 0)
    return jnp.where(inside, block - low + base, SLOTS + 2 * full + (block // 2) % 2)


def q_place(x, j, block):
    job = 16 * j + block
    full = 1 if isinstance(j, int) and j == 1 else jnp.where(j == 1, 1, 0)
    passing = Q_PASS + (2 * full + (block // 2) % 2) * QB
    return jnp.where(pick(job // 6, CHIP_X) == x, (job % 6) // 2 * QB, passing)


def at_rows(ref, first, count, step):
    return ref.at[pl.ds(pl.multiple_of(first, step), count)]


def at_kv(ref, row, count, step):
    return ref.at[row // GROUP, pl.ds(pl.multiple_of(row % GROUP, step), count)]


def whole_kernel(
    table, pkv, pq, attended, d_attended,
    kv0, kv1, kv2, kv3, qq, out, d_out, top, total, light, tilt,
    zs, zqs, ys, yqs, xs, xqs, fs, zr, zqr, yr, yqr, kr, qr, fr, os, dos, orr, dor,
):
    quarters = (kv0, kv1, kv2, kv3)
    block, x, y_hi, y_lo, y, z, core = coordinates()
    side = y % 2
    chip = my_chip(x, y)
    always = block >= 0
    no, both = jnp.logical_not, jnp.logical_and

    barrier = pltpu.get_barrier_semaphore()
    partners = (
        [device(x, y, (z + d) % 4, core) for d in (1, 2, 3)]
        + [device(x, (y + d) % 4, z, core) for d in (1, 2, 3)]
        + [device((x + d) % 4, y, z, core) for d in (1, 2, 3)]
        + [device(x, y, z, 1 - core)]
    )
    for partner in partners:
        pl.semaphore_signal(barrier, inc=1, device_id=partner, device_id_type=MESH)
    own = jnp.int32(0)
    for z_from in range(4):
        for g in range(2):
            for j in range(3):
                owner = (16 * j + block) // 6
                x_from, y_from = pick(owner, CHIP_X), 2 * g + owner // 4
                me = both(both(x_from == x, y_from == y), z == z_from)
                own = own + me.astype(jnp.int32)

                @pl.when(no(me))
                def _():
                    pl.semaphore_signal(
                        barrier, inc=1, device_id=device(x_from, y_from, z_from, core), device_id_type=MESH
                    )

    pl.semaphore_wait(barrier, len(partners) + 24 - own)

    draining = []

    def send(where, source, target, send_sem, recv_sem, to):
        remote = pltpu.make_async_remote_copy(
            src_ref=source, dst_ref=target, send_sem=send_sem, recv_sem=recv_sem, device_id=to, device_id_type=MESH
        )

        @pl.when(where)
        def _():
            if draining:
                remote.wait_send()
            else:
                remote.start()

    def keep(source, target, sem):
        if not draining:
            pltpu.make_async_copy(source, target, sem).start()

    def arrived(where, target, recv_sem):
        if draining:
            return

        @pl.when(where)
        def _():
            pltpu.make_async_copy(target, target, recv_sem).wait()


    def kv_after_z(hh, first, size):
        g, j = hh // 3, hh % 3
        stays = both(y_hi == g, side == j // 2 if j != 1 else wants(side, block))
        in_place = kv_place(x, side, j, block) * GROUP + first + y_lo * (size // 2)
        return jnp.where(stays, in_place, KV_WAIT + hh * (GROUP // 2) + first // 2)

    def q_after_z(hh):
        g, j = hh // 3, hh % 3
        stays = both(y_hi == g, side == (16 * j + block) // 24)
        return stays, jnp.where(stays, q_place(x, j, block) + y_lo * 512, Q_WAIT + hh * 512)

    def z_kv(mid, part, start, size):
        kv, first = quarters[start // GROUP], start % GROUP
        for hh in (1, 4) if mid else (0, 5, 2, 3):
            count = size // 8
            to_rows = at_kv(kv, kv_after_z(hh, first, size) + z * count, count, STEP // 8)
            for d in (2, 1, 3, 0):
                to = (z + d) % 4
                from_rows = pkv.at[6 * to + hh, pl.ds(start // 8, count)]
                if d:
                    send(always, from_rows, to_rows, zs.at[hh, part, d], zr.at[hh, part], device(x, y, to, core))
                else:
                    keep(from_rows, to_rows, zr.at[hh, part])

    def z_q(hh):
        _, row = q_after_z(hh)
        to_rows = at_rows(qq, row + z * CHUNK, CHUNK, CHUNK)
        for d in (2, 1, 3, 0):
            to = (z + d) % 4
            if d:
                send(always, pq.at[6 * to + hh], to_rows, zqs.at[hh, d], zqr.at[hh], device(x, y, to, core))
            else:
                keep(pq.at[6 * to + hh], to_rows, zqr.at[hh])

    def y_kv(mid, part, start, size):
        kv, first = quarters[start // GROUP], start % GROUP
        count = size // 2
        for hh in (1, 4) if mid else (0, 5, 2, 3):
            g, j = hh // 3, hh % 3
            source = at_kv(kv, kv_after_z(hh, first, size), count, STEP // 2)
            arrived(always, source, zr.at[hh, part])
            for s in (0, 1) if mid else (j // 2,):
                where = wants(jnp.int32(s), block) if mid else always
                to = 2 * g + s
                row = kv_place(x, s, j, block) * GROUP + first + y_lo * count
                send(
                    both(where, y != to), source, at_kv(kv, row, count, STEP // 2),
                    ys.at[hh, s, part], yr.at[mid, y_hi, y_lo, part], device(x, to, z, core),
                )

    def y_q(hh):
        g, j = hh // 3, hh % 3
        stays, row = q_after_z(hh)
        source = at_rows(qq, row, 512, 512)
        arrived(always, source, zqr.at[hh])
        send(
            no(stays), source, at_rows(qq, q_place(x, j, block) + y_lo * 512, 512, 512),
            yqs.at[hh], yqr.at[j % 2, y_hi, y_lo], device(x, 2 * g + (16 * j + block) // 24, z, core),
        )

    def x_kv(mid, part, start, size):
        kv, first = quarters[start // GROUP], start % GROUP
        j = 1 if mid else 2 * side
        for t in (0, 1):
            here = 4 * x + 2 * t + core
            came = wants(side, here) if mid else always
            place = kv_place(x, side, j, here)
            row = place * GROUP + first
            for half in (0, 1):
                own = both(t == y_hi, half == y_lo)
                rows = at_kv(kv, row + half * (size // 2), size // 2, STEP // 2)
                arrived(both(came, no(own)), rows, yr.at[mid, t, half, part])
            source = at_kv(kv, row, size, STEP)
            for d in (2, 1, 3):
                to = (x + d) % 4
                low, high, base = window(to, side, j)
                wanted = both(here >= low, here <= high)
                slot = jnp.where(wanted, here - low + base, 0)
                send(
                    wanted, source, at_kv(kv, slot * GROUP + first, size, STEP),
                    xs.at[mid, t, d, part], kr.at[slot, part], device(to, y, z, core),
                )
            kept = both(came, place < SLOTS)
            slot = jnp.where(kept, place, 0)
            rows = at_kv(kv, slot * GROUP + first, size, STEP)
            send(kept, rows, rows, fs.at[mid, t, 0, part], fr.at[slot, part], device(x, y, z, 1 - core))

    def x_q(full_or_mid):
        mid = full_or_mid
        j = 1 if mid else 2 * side
        for t in (0, 1):
            job = 16 * j + 4 * x + 2 * t + core
            owned = job // 24 == side
            row = q_place(x, j, 4 * x + 2 * t + core)
            for half in (0, 1):
                own = both(t == y_hi, half == y_lo)
                arrived(both(owned, no(own)), at_rows(qq, row + half * 512, 512, 512), yqr.at[mid, t, half])
            to = pick(job // 6, CHIP_X)
            slot = (job % 6) // 2
            send(
                both(owned, to != x), at_rows(qq, row, QB, QB), at_rows(qq, slot * QB, QB, QB),
                xqs.at[mid, t], qr.at[slot], device(to, y, z, core),
            )

    def wanted_here(mid, t, d, other):
        low, high, base = window(x, side, 1 if mid else 2 * side)
        from_block = 4 * ((x + d) % 4) + 2 * t + (1 - core if other else core)
        wanted = both(from_block >= low, from_block <= high)
        return wanted, jnp.where(wanted, from_block - low + base, 0)

    def to_other_core(mid, part, start, size):
        kv, first = quarters[start // GROUP], start % GROUP
        for d in (1, 3, 2):
            for t in (0, 1):
                wanted, slot = wanted_here(mid, t, d, False)
                rows = at_kv(kv, slot * GROUP + first, size, STEP)
                arrived(wanted, rows, kr.at[slot, part])
                send(wanted, rows, rows, fs.at[mid, t, d, part], fr.at[slot, part], device(x, y, z, 1 - core))

    stages = {"z": z_kv, "y": y_kv, "x": x_kv, "c": to_other_core}
    stages_q = {"z": z_q, "y": y_q, "x": x_q}

    def go(step):
        name, item = step
        if isinstance(item, tuple):
            for mid in (0, 1):
                stages[name](mid, *item)
        else:
            stages_q[name](item)

    def complete(part, start, size):
        kv, first = quarters[start // GROUP], start % GROUP
        for mid, t in ((0, 0), (0, 1), (1, 0), (1, 1)):
            for d in (0, 1, 3, 2):
                wanted, slot = wanted_here(mid, t, d, True)
                arrived(wanted, at_kv(kv, slot * GROUP + first, size, STEP), fr.at[slot, part])

    def attend(quarter, tile):
        i = tile // (QB // TILE)
        at = pl.ds(pl.multiple_of(tile * TILE, TILE), TILE)
        kv = quarters[quarter]
        held = [kv[table[i, s]] for s in range(5)]
        absent = [jnp.where(table[3 + i, s] == 1, 0.0, 1e32) for s in range(5)]
        both_keys = jnp.concatenate([block_rows[:, 0:256] for block_rows in held], axis=0)
        both_values = jnp.concatenate([block_rows[:, 256:512] for block_rows in held], axis=0)
        ones = jnp.ones((5 * GROUP, 128), jnp.bfloat16)
        values = jnp.concatenate([both_values[:, 0:128], ones], axis=1)
        across = (((1,), (1,)), ((), ()))
        rows = qq[at, :]
        score = lax.dot_general(
            rows[:, 128:256], both_keys[:, 0:128], across, preferred_element_type=jnp.float32
        )
        d_score = lax.dot_general(rows, both_keys, across, preferred_element_type=jnp.float32)
        parts = [score[:, s * GROUP : (s + 1) * GROUP] for s in range(5)]
        tops = [jnp.max(parts[s], axis=1, keepdims=True) - absent[s] for s in range(5)]
        peak = functools.reduce(jnp.maximum, tops)
        if quarter:
            old = top[at, :]
            new = jnp.maximum(old, peak)
            fade = jnp.exp2((old - new) * (SCALE * LOG2E))
            fade2 = jnp.concatenate([fade, fade], axis=1)
        else:
            new = jnp.broadcast_to(peak, (TILE, 128))
        weight = jnp.concatenate(
            [jnp.exp2((parts[s] - (new[:, 0:1] + absent[s])) * (SCALE * LOG2E)) for s in range(5)], axis=1
        )
        tilted = weight * d_score
        sums = weight[:, 0:128]
        for c in range(1, 5 * GROUP // 128):
            sums = sums + weight[:, 128 * c : 128 * c + 128]
        lit = jnp.dot(weight.astype(jnp.bfloat16), both_values, preferred_element_type=jnp.float32)
        leaned = jnp.dot(tilted.astype(jnp.bfloat16), values, preferred_element_type=jnp.float32)
        if quarter:
            sums = total[at, :] * fade + sums
            lit = light[at, :] * fade2 + lit
            leaned = tilt[at, :] * fade2 + leaned
        if quarter < 3:
            top[at, :] = new
            total[at, :] = sums
            light[at, :] = lit
            tilt[at, :] = leaned
        else:
            inverse = 1.0 / jnp.sum(sums, axis=1, keepdims=True)
            result = lit[:, 0:128] * inverse
            moved = lit[:, 128:256] + SCALE * leaned[:, 0:128]
            slope = SCALE * leaned[:, 128:256]
            out[at, :] = result.astype(jnp.bfloat16)
            d_out[at, :] = (moved * inverse - slope * inverse * result).astype(jnp.bfloat16)

    def give_back(i):
        job = 6 * chip + 2 * i + core
        j, b = job // 16, job % 16
        lanes = pl.ds(pl.multiple_of((6 * z + 3 * (y // 2) + j) * 128, 128), 128)
        for d in range(8):
            p = (d + 4 * y_lo + z) % 8
            me = both(b == block, p == 4 * y_lo + z)
            for source, target, sends, recv in ((out, attended, os, orr), (d_out, d_attended, dos, dor)):
                from_ref, to_ref = at_rows(source, i * QB + p * CHUNK, CHUNK, CHUNK), target.at[:, lanes]
                if not draining:

                    @pl.when(me)
                    def _():
                        pltpu.make_async_copy(from_ref, to_ref, recv).start()

                send(no(me), from_ref, to_ref, sends.at[i, d], recv, (b, p))

    for quarter in range(4):
        before, during = SCHEDULE[quarter]
        for step in before:
            go(step)
        if quarter == 0:
            for i in range(3):
                b = (6 * chip + 2 * i + core) % 16
                arrived(b // 4 != x, at_rows(qq, i * QB, QB, QB), qr.at[i])
        for part, start, size in PARTS:
            if start // GROUP == quarter:
                complete(part, start, size)

        @pl.loop(0, 3 * QB // TILE)
        def _(tile):
            attend(quarter, tile)
            for turn, step in during:

                @pl.when(tile == turn)
                def _():
                    go(step)

            if quarter == 3:

                @pl.when(tile % (QB // TILE) == QB // TILE - 1)
                def _():
                    give_back(tile // (QB // TILE))

    pltpu.make_async_copy(attended, attended, orr).wait()
    pltpu.make_async_copy(d_attended, d_attended, dor).wait()
    draining.append(True)
    for before, during in SCHEDULE:
        for step in before + [step for _, step in during]:
            go(step)

    @pl.loop(0, 3)
    def _(i):
        give_back(i)


STEP = 128
TILE = 512
SIZES = (128, 128, 256, 256, 256)
PARTS = [(part, sum(SIZES[:part]), size) for part, size in enumerate(SIZES)]


def make_schedule(lead=3, lag_x=1, lag_c=3):
    kv = [("kv", part) for part in PARTS]
    queries = [("q", pair) for pair in ((0, 5), (2, 3), (1, 4))]
    steps = [kv[0], queries[0], kv[1], queries[1], kv[2], queries[2], kv[3], kv[4]]

    def one(stage, index):
        if not 0 <= index < len(steps):
            return []
        kind, item = steps[index]
        if kind == "kv":
            return [(stage, item)]
        if stage in "zy":
            return [(stage, hh) for hh in item]
        if stage == "x" and index == 3:
            return [("x", 0)]
        if stage == "x" and index == 5:
            return [("x", 1)]
        return []

    def turn(step):
        return one("y", step) + one("z", step + lead) + one("x", step - lag_x) + one("c", step - lag_c)

    first = [step for i in range(lead) for step in one("z", i)]
    for i in range(7):
        first += turn(i)
    y7, x6, c4 = one("y", 7), one("x", 6), one("c", 4)
    x7, c6, c7 = one("x", 7), one("c", 6), one("c", 7)
    return [
        (first, [(0, step) for step in y7] + [(1, step) for step in x6] + [(3, step) for step in c4]),
        ([], [(0, step) for step in x7] + [(3, step) for step in c6]),
        ([], [(3, step) for step in c7]),
        ([], []),
    ]


SCHEDULE = make_schedule()


def bring_attend_return(table, pkv, pq):
    anywhere = pl.BlockSpec(memory_space=pl.ANY)
    dma, vmem = pltpu.SemaphoreType.DMA, pltpu.VMEM
    n = len(PARTS)
    sems = [
        (6, n, 4), (6, 4), (6, 2, n), (6,), (2, 2, 4, n), (2, 2), (2, 2, 4, n),
        (6, n), (6,), (2, 2, 2, n), (2, 2, 2), (SLOTS, n), (3,), (SLOTS, n), (3, 8), (3, 8),
    ]
    return pl.pallas_call(
        whole_kernel,
        name="bring_attend_return",
        out_shape=(jax.ShapeDtypeStruct((CHUNK, 3072), jnp.bfloat16),) * 2,
        in_specs=[pl.BlockSpec(memory_space=pltpu.SMEM), anywhere, anywhere],
        out_specs=(anywhere,) * 2,
        scratch_shapes=[vmem((SLOTS + 7, GROUP, 512), jnp.bfloat16)] * 4
        + [vmem((Q_ROWS, 256), jnp.bfloat16)]
        + [vmem((3 * QB, 128), jnp.bfloat16)] * 2
        + [vmem((3 * QB, 128), jnp.float32)] * 2
        + [vmem((3 * QB, 256), jnp.float32)] * 2
        + [dma(shape) for shape in sems]
        + [dma, dma],
        compiler_params=pltpu.CompilerParams(
            collective_id=0, has_side_effects=True, vmem_limit_bytes=62 * 2**20
        ),
    )(table, pkv, pq)


def on_device(queries, keys, values, d_queries, d_keys, d_values, positions, key_lists):
    pkv, pq, table = rotate_all(queries, keys, values, d_queries, d_keys, d_values, positions, key_lists)
    return bring_attend_return(table, pkv, pq)


def solution(mesh):
    tokens = P(("blk", "head"), None)
    return jax.shard_map(
        on_device,
        mesh=mesh,
        in_specs=(tokens,) * 6 + (P(None, ("blk", "head")), P()),
        out_specs=(tokens, tokens),
        check_vma=False,
    )
```

```python
import functools

import jax
import jax.numpy as jnp
import numpy as np
from jax import lax
from jax.experimental import pallas as pl
from jax.experimental.pallas import tpu as pltpu
from jax.sharding import PartitionSpec as P

MESH = pl.DeviceIdType.MESH
REACH = 3
BLOCKS = 16
CHUNK = 128
QB = 1024
SCALE = 128 ** (-0.5)
LOG2E = 1.4426950408889634
CHIP_X = (0, 2, 3, 1, 2, 0, 1, 3)
SLOTS = 12


def chip_runs():
    runs = []
    for k in range(8):
        mine, base = [], 0
        for j in range(3):
            blocks = [job % 16 for job in range(6 * k, 6 * k + 6) if job // 16 == j]
            if blocks:
                low, high = max(0, blocks[0] - REACH), min(BLOCKS - 1, blocks[-1] + REACH)
                mine.append((j, low, high, base))
                base += high - low + 1
        runs.append(mine)
    return runs


RUNS = chip_runs()
CHIP_AT = [[CHIP_X[4 * side : 4 * side + 4].index(x) + 4 * side for x in range(4)] for side in range(2)]


def pick(index, values):
    result = jnp.int32(values[0])
    for place, value in enumerate(values[1:], 1):
        if value != values[0]:
            result = jnp.where(index == place, jnp.int32(value), result)
    return result


def run_code(k, j):
    for head, low, high, base in RUNS[k]:
        if head == j:
            return (low * 64 + high) * 64 + base
    return (63 * 64) * 64


def coordinates():
    block = lax.axis_index("blk")
    part = lax.axis_index("head")
    x, y_hi, core = block // 4, (block // 2) % 2, block % 2
    y_lo, z = part // 4, part % 4
    return block, x, y_hi, y_lo, 2 * y_hi + y_lo, z, core


def device(x, y, z, core):
    return (4 * x + 2 * (y // 2) + core, 4 * (y % 2) + z)


def my_chip(x, y):
    return pick(4 * (y % 2) + x, CHIP_AT[0] + CHIP_AT[1])


def frequency_rows():
    tables = np.zeros((3, 128), np.float32)
    start = 0
    for axis_id, count, span in ((0, 22, 44), (1, 21, 42), (2, 21, 42)):
        for column in range(count):
            rate = 1.0 / 10000.0 ** (2.0 * column / span)
            tables[axis_id, 2 * (start + column)] = rate
            tables[axis_id, 2 * (start + column) + 1] = rate
        start += count
    return tables


def swap_table():
    table = np.zeros((128, 128), np.float32)
    for pair in range(64):
        table[2 * pair + 1, 2 * pair] = -1.0
        table[2 * pair, 2 * pair + 1] = 1.0
    return table


def rotate_kernel(
    lists_ref, spots_ref, rates_ref, swap_ref, q_ref, k_ref, v_ref, dq_ref, dk_ref, dv_ref,
    kv_ref, qq_ref, table_ref, cos_ref, sin_ref,
):
    heads = kv_ref.shape[0]

    @pl.when(pl.program_id(0) == 0)
    def _():
        spots = spots_ref[...].astype(jnp.float32)
        angle = jnp.zeros((CHUNK, 128), jnp.float32)
        for axis_id in range(3):
            column = jnp.broadcast_to(spots[axis_id : axis_id + 1, :], (128, CHUNK)).T
            angle = angle + column * rates_ref[axis_id : axis_id + 1, :]
        cos_ref[...] = jnp.cos(angle)
        sin_ref[...] = jnp.sin(angle)
        _, x, _, _, y, _, core = coordinates()
        chip = my_chip(x, y)
        for i in range(3):
            job = 6 * chip + 2 * i + core
            j, block = job // 16, job % 16
            code = pick(3 * chip + j, [run_code(k, h) for k in range(8) for h in range(3)])
            low, base = code // 4096, code % 64
            last = jnp.int32(0)
            for s in range(5):
                entry = lists_ref[block, s]
                listed = entry >= 0
                last = jnp.where(listed, entry - low + base, last)
                table_ref[i, s] = last
                table_ref[3 + i, s] = listed.astype(jnp.int32)

    cosine, sine, swap = cos_ref[...], sin_ref[...], swap_ref[...]

    def turned(ref, lanes):
        part = ref[:, lanes]
        swapped = jnp.dot(part, swap, preferred_element_type=jnp.float32)
        return (part.astype(jnp.float32) * cosine + swapped * sine).astype(jnp.bfloat16)

    for head in range(heads):
        lanes = slice(128 * head, 128 * head + 128)
        kv_ref[head, :, 0:128] = turned(k_ref, lanes)
        kv_ref[head, :, 128:256] = turned(dk_ref, lanes)
        kv_ref[head, :, 256:384] = v_ref[:, lanes]
        kv_ref[head, :, 384:512] = dv_ref[:, lanes]
        qq_ref[head, :, 0:128] = turned(dq_ref, lanes)
        qq_ref[head, :, 128:256] = turned(q_ref, lanes)


def rotate_all(queries, keys, values, d_queries, d_keys, d_values, positions, key_lists):
    group = 4
    steps = 24 // group
    whole = pl.BlockSpec(memory_space=pltpu.VMEM)
    columns = pl.BlockSpec((CHUNK, 128 * group), lambda i: (0, i))
    return pl.pallas_call(
        rotate_kernel,
        name="rotate",
        grid=(steps,),
        out_shape=(
            jax.ShapeDtypeStruct((24, CHUNK, 512), jnp.bfloat16),
            jax.ShapeDtypeStruct((24, CHUNK, 256), jnp.bfloat16),
            jax.ShapeDtypeStruct((6, 5), jnp.int32),
        ),
        in_specs=[pl.BlockSpec(memory_space=pltpu.SMEM), whole, whole, whole] + [columns] * 6,
        out_specs=(
            pl.BlockSpec((group, CHUNK, 512), lambda i: (i, 0, 0)),
            pl.BlockSpec((group, CHUNK, 256), lambda i: (i, 0, 0)),
            pl.BlockSpec(memory_space=pltpu.SMEM),
        ),
        scratch_shapes=[pltpu.VMEM((CHUNK, 128), jnp.float32)] * 2,
        compiler_params=pltpu.CompilerParams(vmem_limit_bytes=62 * 2**20),
    )(
        key_lists, positions, jnp.asarray(frequency_rows()), jnp.asarray(swap_table(), jnp.bfloat16),
        queries, keys, values, d_queries, d_keys, d_values,
    )


GROUP = 256
KV_WAIT = (SLOTS + 4) * GROUP
Q_PASS, Q_WAIT, Q_ROWS = 3 * QB, 7 * QB, 10 * QB
CODES = [run_code(CHIP_AT[side][x], j) for j in range(3) for side in range(2) for x in range(4)]


def window(x, side, j):
    code = pick(8 * j + 4 * side + x, CODES)
    return code // 4096, (code // 64) % 64, code % 64


def wants(side, block):
    return jnp.where(side == 0, block <= 10, block >= 5)


def kv_place(x, side, j, block):
    low, high, base = window(x, side, j)
    inside = jnp.logical_and(block >= low, block <= high)
    full = 1 if isinstance(j, int) and j == 1 else jnp.where(j == 1, 1, 0)
    return jnp.where(inside, block - low + base, SLOTS + 2 * full + (block // 2) % 2)


def q_place(x, j, block):
    job = 16 * j + block
    full = 1 if isinstance(j, int) and j == 1 else jnp.where(j == 1, 1, 0)
    passing = Q_PASS + (2 * full + (block // 2) % 2) * QB
    return jnp.where(pick(job // 6, CHIP_X) == x, (job % 6) // 2 * QB, passing)


def at_rows(ref, first, count, step):
    return ref.at[pl.ds(pl.multiple_of(first, step), count)]


def at_kv(ref, row, count, step):
    return ref.at[row // GROUP, pl.ds(pl.multiple_of(row % GROUP, step), count)]


def whole_kernel(
    table, pkv, pq, results,
    kv0, kv1, kv2, kv3, qq, out, top, total, light, tilt,
    zs, zqs, ys, yqs, xs, xqs, fs, zr, zqr, yr, yqr, kr, qr, fr, os, done,
):
    quarters = (kv0, kv1, kv2, kv3)
    block, x, y_hi, y_lo, y, z, core = coordinates()
    side = y % 2
    chip = my_chip(x, y)
    always = block >= 0
    no, both = jnp.logical_not, jnp.logical_and

    barrier = pltpu.get_barrier_semaphore()
    partners = (
        [device(x, y, (z + d) % 4, core) for d in (1, 2, 3)]
        + [device(x, (y + d) % 4, z, core) for d in (1, 2, 3)]
        + [device((x + d) % 4, y, z, core) for d in (1, 2, 3)]
        + [device(x, y, z, 1 - core)]
    )
    for partner in partners:
        pl.semaphore_signal(barrier, inc=1, device_id=partner, device_id_type=MESH)
    own = jnp.int32(0)
    for z_from in range(4):
        for g in range(2):
            for j in range(3):
                owner = (16 * j + block) // 6
                x_from, y_from = pick(owner, CHIP_X), 2 * g + owner // 4
                me = both(both(x_from == x, y_from == y), z == z_from)
                own = own + me.astype(jnp.int32)

                @pl.when(no(me))
                def _():
                    pl.semaphore_signal(
                        barrier, inc=1, device_id=device(x_from, y_from, z_from, core), device_id_type=MESH
                    )

    pl.semaphore_wait(barrier, len(partners) + 24 - own)

    draining = []

    def send(where, source, target, send_sem, recv_sem, to):
        remote = pltpu.make_async_remote_copy(
            src_ref=source, dst_ref=target, send_sem=send_sem, recv_sem=recv_sem, device_id=to, device_id_type=MESH
        )

        @pl.when(where)
        def _():
            if draining:
                remote.wait_send()
            else:
                remote.start()

    def keep(source, target, sem):
        if not draining:
            pltpu.make_async_copy(source, target, sem).start()

    def arrived(where, target, recv_sem):
        if draining:
            return

        @pl.when(where)
        def _():
            pltpu.make_async_copy(target, target, recv_sem).wait()


    def kv_after_z(hh, first, size):
        g, j = hh // 3, hh % 3
        stays = both(y_hi == g, side == j // 2 if j != 1 else wants(side, block))
        in_place = kv_place(x, side, j, block) * GROUP + first + y_lo * (size // 2)
        return jnp.where(stays, in_place, KV_WAIT + hh * (GROUP // 2) + first // 2)

    def head_of(place, b):
        return (2 * (place + 3 - (b // 2) % 3)) % 3

    def q_after_z(place, g):
        j = head_of(place, block)
        stays = both(y_hi == g, side == (16 * j + block) // 24)
        row = jnp.where(stays, q_place(x, j, block) + y_lo * 512, Q_WAIT + (3 * g + j) * 512)
        return j, stays, row

    def z_kv(mid, part, start, size):
        kv, first = quarters[start // GROUP], start % GROUP
        for hh in (1, 4) if mid else (0, 5, 2, 3):
            count = size // 8
            to_rows = at_kv(kv, kv_after_z(hh, first, size) + z * count, count, STEP // 8)
            for d in (2, 1, 3, 0):
                to = (z + d) % 4
                from_rows = pkv.at[6 * to + hh, pl.ds(start // 8, count)]
                if d:
                    send(always, from_rows, to_rows, zs.at[hh, part, d], zr.at[hh, part], device(x, y, to, core))
                else:
                    keep(from_rows, to_rows, zr.at[hh, part])

    def z_q(place):
        for g in range(2):
            j, _, row = q_after_z(place, g)
            to_rows = at_rows(qq, row + z * CHUNK, CHUNK, CHUNK)
            for d in (2, 1, 3, 0):
                to = (z + d) % 4
                from_rows = pq.at[6 * to + 3 * g + j]
                if d:
                    send(
                        always, from_rows, to_rows, zqs.at[place, g, d], zqr.at[place, g], device(x, y, to, core)
                    )
                else:
                    keep(from_rows, to_rows, zqr.at[place, g])

    def y_kv(mid, part, start, size):
        kv, first = quarters[start // GROUP], start % GROUP
        count = size // 2
        for hh in (1, 4) if mid else (0, 5, 2, 3):
            g, j = hh // 3, hh % 3
            source = at_kv(kv, kv_after_z(hh, first, size), count, STEP // 2)
            arrived(always, source, zr.at[hh, part])
            for s in (0, 1) if mid else (j // 2,):
                where = wants(jnp.int32(s), block) if mid else always
                to = 2 * g + s
                row = kv_place(x, s, j, block) * GROUP + first + y_lo * count
                send(
                    both(where, y != to), source, at_kv(kv, row, count, STEP // 2),
                    ys.at[hh, s, part], yr.at[mid, y_hi, y_lo, part], device(x, to, z, core),
                )

    def y_q(place):
        for g in range(2):
            j, stays, row = q_after_z(place, g)
            source = at_rows(qq, row, 512, 512)
            arrived(always, source, zqr.at[place, g])
            send(
                no(stays), source, at_rows(qq, q_place(x, j, block) + y_lo * 512, 512, 512),
                yqs.at[place, g], yqr.at[place, y_hi, y_lo], device(x, 2 * g + (16 * j + block) // 24, z, core),
            )

    def x_kv(mid, part, start, size):
        kv, first = quarters[start // GROUP], start % GROUP
        j = 1 if mid else 2 * side
        for t in (0, 1):
            here = 4 * x + 2 * t + core
            came = wants(side, here) if mid else always
            place = kv_place(x, side, j, here)
            row = place * GROUP + first
            for half in (0, 1):
                own = both(t == y_hi, half == y_lo)
                rows = at_kv(kv, row + half * (size // 2), size // 2, STEP // 2)
                arrived(both(came, no(own)), rows, yr.at[mid, t, half, part])
            source = at_kv(kv, row, size, STEP)
            for d in (2, 1, 3):
                to = (x + d) % 4
                low, high, base = window(to, side, j)
                wanted = both(here >= low, here <= high)
                slot = jnp.where(wanted, here - low + base, 0)
                send(
                    wanted, source, at_kv(kv, slot * GROUP + first, size, STEP),
                    xs.at[mid, t, d, part], kr.at[slot, part], device(to, y, z, core),
                )
            kept = both(came, place < SLOTS)
            slot = jnp.where(kept, place, 0)
            rows = at_kv(kv, slot * GROUP + first, size, STEP)
            send(kept, rows, rows, fs.at[mid, t, 0, part], fr.at[slot, part], device(x, y, z, 1 - core))

    def x_q(place):
        for t in (0, 1):
            here = 4 * x + 2 * t + core
            j = head_of(place, here)
            job = 16 * j + here
            owned = job // 24 == side
            row = q_place(x, j, here)
            for half in (0, 1):
                own = both(t == y_hi, half == y_lo)
                arrived(both(owned, no(own)), at_rows(qq, row + half * 512, 512, 512), yqr.at[place, t, half])
            to = pick(job // 6, CHIP_X)
            send(
                both(owned, to != x), at_rows(qq, row, QB, QB), at_rows(qq, place * QB, QB, QB),
                xqs.at[place, t], qr.at[place], device(to, y, z, core),
            )

    def wanted_here(mid, t, d, other):
        low, high, base = window(x, side, 1 if mid else 2 * side)
        from_block = 4 * ((x + d) % 4) + 2 * t + (1 - core if other else core)
        wanted = both(from_block >= low, from_block <= high)
        return wanted, jnp.where(wanted, from_block - low + base, 0)

    def to_other_core(mid, part, start, size):
        kv, first = quarters[start // GROUP], start % GROUP
        for d in (1, 3, 2):
            for t in (0, 1):
                wanted, slot = wanted_here(mid, t, d, False)
                rows = at_kv(kv, slot * GROUP + first, size, STEP)
                arrived(wanted, rows, kr.at[slot, part])
                send(wanted, rows, rows, fs.at[mid, t, d, part], fr.at[slot, part], device(x, y, z, 1 - core))

    stages = {"z": z_kv, "y": y_kv, "x": x_kv, "c": to_other_core}
    stages_q = {"z": z_q, "y": y_q, "x": x_q}

    def go(step):
        name, item = step
        if isinstance(item, tuple):
            for mid in (0, 1):
                stages[name](mid, *item)
        else:
            stages_q[name](item)

    def complete(part, start, size):
        kv, first = quarters[start // GROUP], start % GROUP
        for mid, t in ((0, 0), (0, 1), (1, 0), (1, 1)):
            for d in (0, 1, 3, 2):
                wanted, slot = wanted_here(mid, t, d, True)
                arrived(wanted, at_kv(kv, slot * GROUP + first, size, STEP), fr.at[slot, part])

    def attend(quarter, i):
        at = pl.ds(pl.multiple_of(i * QB, QB), QB)
        kv = quarters[quarter]
        held = [kv[table[i, s]] for s in range(5)]
        absent = [jnp.where(table[3 + i, s] == 1, 0.0, 1e32) for s in range(5)]
        both_keys = jnp.concatenate([block_rows[:, 0:256] for block_rows in held], axis=0)
        both_values = jnp.concatenate([block_rows[:, 256:512] for block_rows in held], axis=0)
        ones = jnp.ones((5 * GROUP, 128), jnp.bfloat16)
        values = jnp.concatenate([both_values[:, 0:128], ones], axis=1)
        across = (((1,), (1,)), ((), ()))
        rows = qq[at, :]
        score = lax.dot_general(
            rows[:, 128:256], both_keys[:, 0:128], across, preferred_element_type=jnp.float32
        )
        d_score = lax.dot_general(rows, both_keys, across, preferred_element_type=jnp.float32)
        parts = [score[:, s * GROUP : (s + 1) * GROUP] for s in range(5)]
        tops = [jnp.max(parts[s], axis=1, keepdims=True) - absent[s] for s in range(5)]
        peak = functools.reduce(jnp.maximum, tops)
        if quarter:
            old = top[at, :]
            new = jnp.maximum(old, peak)
            fade = jnp.exp2((old - new) * (SCALE * LOG2E))
            fade2 = jnp.concatenate([fade, fade], axis=1)
        else:
            new = jnp.broadcast_to(peak, (QB, 128))
        weight = jnp.concatenate(
            [jnp.exp2((parts[s] - (new[:, 0:1] + absent[s])) * (SCALE * LOG2E)) for s in range(5)], axis=1
        )
        tilted = weight * d_score
        sums = weight[:, 0:128]
        for c in range(1, 5 * GROUP // 128):
            sums = sums + weight[:, 128 * c : 128 * c + 128]
        lit = jnp.dot(weight.astype(jnp.bfloat16), both_values, preferred_element_type=jnp.float32)
        leaned = jnp.dot(tilted.astype(jnp.bfloat16), values, preferred_element_type=jnp.float32)
        if quarter:
            sums = total[at, :] * fade + sums
            lit = light[at, :] * fade2 + lit
            leaned = tilt[at, :] * fade2 + leaned
        if quarter < 3:
            top[at, :] = new
            total[at, :] = sums
            light[at, :] = lit
            tilt[at, :] = leaned
        else:
            inverse = 1.0 / jnp.sum(sums, axis=1, keepdims=True)
            result = lit[:, 0:128] * inverse
            moved = lit[:, 128:256] + SCALE * leaned[:, 0:128]
            slope = SCALE * leaned[:, 128:256]
            out[at, 0:128] = result.astype(jnp.bfloat16)
            out[at, 128:256] = (moved * inverse - slope * inverse * result).astype(jnp.bfloat16)

    def give_back(i):
        job = 6 * chip + 2 * i + core
        j, b = job // 16, job % 16
        head = 6 * z + 3 * (y // 2) + j
        for d in range(8):
            p = (d + 4 * y_lo + z) % 8
            me = both(b == block, p == 4 * y_lo + z)
            from_ref, to_ref = at_rows(out, i * QB + p * CHUNK, CHUNK, CHUNK), results.at[head]
            if not draining:

                @pl.when(me)
                def _():
                    pltpu.make_async_copy(from_ref, to_ref, done).start()

            send(no(me), from_ref, to_ref, os.at[i, d], done, (b, p))

    first, between = PROGRAM
    for step in first:
        go(step)

    @pl.loop(0, 3)
    def _(i):
        b = (6 * chip + 2 * i + core) % 16
        arrived(b // 4 != x, at_rows(qq, i * QB, QB, QB), qr.at[i])
        for quarter in range(4):

            @pl.when(i == 0)
            def _():
                for step in between[quarter]:
                    go(step)
                for part, start, size in PARTS:
                    if start // GROUP == quarter:
                        complete(part, start, size)

            attend(quarter, i)
        give_back(i)

    pltpu.make_async_copy(results, results, done).wait()
    draining.append(True)
    for step in first + between[0] + between[1] + between[2] + between[3]:
        go(step)

    @pl.loop(0, 3)
    def _(i):
        give_back(i)


STEP = 128
SIZES = (128, 128, 256, 256, 256)
PARTS = [(part, sum(SIZES[:part]), size) for part, size in enumerate(SIZES)]


def make_program(order, lead, lag_x, lag_c, before, where):
    steps = [PARTS[int(c)] if c.isdigit() else "abc".index(c) for c in order]

    def one(stage, index):
        if not 0 <= index < len(steps) or (stage == "c" and not isinstance(steps[index], tuple)):
            return []
        return [(stage, steps[index])]

    first = [step for i in range(lead) for step in one("z", i)]
    turns = [
        one("y", turn) + one("z", turn + lead) + one("x", turn - lag_x) + one("c", turn - lag_c)
        for turn in range(len(steps) + max(lag_x, lag_c))
    ]
    for turn in turns[:before]:
        first += turn
    between = [[] for _ in range(4)]
    for place, turn in zip(where, turns[before:]):
        between[place] += turn
    return first, between


PROGRAM = make_program("01234abc", 3, 1, 3, 7, (1, 2, 3, 3))


def bring_attend_return(table, pkv, pq):
    anywhere = pl.BlockSpec(memory_space=pl.ANY)
    dma, vmem = pltpu.SemaphoreType.DMA, pltpu.VMEM
    n = len(PARTS)
    sems = [
        (6, n, 4), (3, 2, 4), (6, 2, n), (3, 2), (2, 2, 4, n), (3, 2), (2, 2, 4, n),
        (6, n), (3, 2), (2, 2, 2, n), (3, 2, 2), (SLOTS, n), (3,), (SLOTS, n), (3, 8),
    ]
    return pl.pallas_call(
        whole_kernel,
        name="bring_attend_return",
        out_shape=jax.ShapeDtypeStruct((24, CHUNK, 256), jnp.bfloat16),
        in_specs=[pl.BlockSpec(memory_space=pltpu.SMEM), anywhere, anywhere],
        out_specs=anywhere,
        scratch_shapes=[vmem((SLOTS + 7, GROUP, 512), jnp.bfloat16)] * 4
        + [vmem((Q_ROWS, 256), jnp.bfloat16)]
        + [vmem((3 * QB, 256), jnp.bfloat16)]
        + [vmem((3 * QB, 128), jnp.float32)] * 2
        + [vmem((3 * QB, 256), jnp.float32)] * 2
        + [dma(shape) for shape in sems]
        + [dma],
        compiler_params=pltpu.CompilerParams(
            collective_id=0, has_side_effects=True, vmem_limit_bytes=62 * 2**20
        ),
    )(table, pkv, pq)


def on_device(queries, keys, values, d_queries, d_keys, d_values, positions, key_lists):
    pkv, pq, table = rotate_all(queries, keys, values, d_queries, d_keys, d_values, positions, key_lists)
    by_head = bring_attend_return(table, pkv, pq)
    return tuple(
        by_head[:, :, first : first + 128].transpose(1, 0, 2).reshape(CHUNK, 3072) for first in (0, 128)
    )


def solution(mesh):
    tokens = P(("blk", "head"), None)
    return jax.shard_map(
        on_device,
        mesh=mesh,
        in_specs=(tokens,) * 6 + (P(None, ("blk", "head")), P()),
        out_specs=(tokens, tokens),
        check_vma=False,
    )
```

```python
import functools

import jax
import jax.numpy as jnp
import numpy as np
from jax import lax
from jax.experimental import pallas as pl
from jax.experimental.pallas import tpu as pltpu
from jax.sharding import PartitionSpec as P

MESH = pl.DeviceIdType.MESH
REACH = 3
BLOCKS = 16
CHUNK = 128
QB = 1024
SCALE = 128 ** (-0.5)
LOG2E = 1.4426950408889634
CHIP_X = (0, 2, 3, 1, 2, 0, 1, 3)
SLOTS = 12


def chip_runs():
    runs = []
    for k in range(8):
        mine, base = [], 0
        for j in range(3):
            blocks = [job % 16 for job in range(6 * k, 6 * k + 6) if job // 16 == j]
            if blocks:
                low, high = max(0, blocks[0] - REACH), min(BLOCKS - 1, blocks[-1] + REACH)
                mine.append((j, low, high, base))
                base += high - low + 1
        runs.append(mine)
    return runs


RUNS = chip_runs()
CHIP_AT = [[CHIP_X[4 * side : 4 * side + 4].index(x) + 4 * side for x in range(4)] for side in range(2)]


def pick(index, values):
    result = jnp.int32(values[0])
    for place, value in enumerate(values[1:], 1):
        if value != values[0]:
            result = jnp.where(index == place, jnp.int32(value), result)
    return result


def run_code(k, j):
    for head, low, high, base in RUNS[k]:
        if head == j:
            return (low * 64 + high) * 64 + base
    return (63 * 64) * 64


def coordinates():
    block = lax.axis_index("blk")
    part = lax.axis_index("head")
    x, y_hi, core = block // 4, (block // 2) % 2, block % 2
    y_lo, z = part // 4, part % 4
    return block, x, y_hi, y_lo, 2 * y_hi + y_lo, z, core


def device(x, y, z, core):
    return (4 * x + 2 * (y // 2) + core, 4 * (y % 2) + z)


def my_chip(x, y):
    return pick(4 * (y % 2) + x, CHIP_AT[0] + CHIP_AT[1])


def frequency_rows():
    tables = np.zeros((3, 128), np.float32)
    start = 0
    for axis_id, count, span in ((0, 22, 44), (1, 21, 42), (2, 21, 42)):
        for column in range(count):
            rate = 1.0 / 10000.0 ** (2.0 * column / span)
            tables[axis_id, 2 * (start + column)] = rate
            tables[axis_id, 2 * (start + column) + 1] = rate
        start += count
    return tables


def swap_table():
    table = np.zeros((128, 128), np.float32)
    for pair in range(64):
        table[2 * pair + 1, 2 * pair] = -1.0
        table[2 * pair, 2 * pair + 1] = 1.0
    return table


def rotate_kernel(
    lists_ref, spots_ref, rates_ref, swap_ref, q_ref, k_ref, v_ref, dq_ref, dk_ref, dv_ref,
    kv_ref, qq_ref, table_ref, cos_ref, sin_ref,
):
    heads = kv_ref.shape[0]

    @pl.when(pl.program_id(0) == 0)
    def _():
        spots = spots_ref[...].astype(jnp.float32)
        angle = jnp.zeros((CHUNK, 128), jnp.float32)
        for axis_id in range(3):
            column = jnp.broadcast_to(spots[axis_id : axis_id + 1, :], (128, CHUNK)).T
            angle = angle + column * rates_ref[axis_id : axis_id + 1, :]
        cos_ref[...] = jnp.cos(angle)
        sin_ref[...] = jnp.sin(angle)
        _, x, _, _, y, _, core = coordinates()
        chip = my_chip(x, y)
        for i in range(3):
            job = 6 * chip + 2 * i + core
            j, block = job // 16, job % 16
            code = pick(3 * chip + j, [run_code(k, h) for k in range(8) for h in range(3)])
            low, base = code // 4096, code % 64
            last = jnp.int32(0)
            for s in range(5):
                entry = lists_ref[block, s]
                listed = entry >= 0
                last = jnp.where(listed, entry - low + base, last)
                table_ref[i, s] = last
                table_ref[3 + i, s] = listed.astype(jnp.int32)

    cosine, sine, swap = cos_ref[...], sin_ref[...], swap_ref[...]

    def turned(ref, lanes):
        part = ref[:, lanes]
        swapped = jnp.dot(part, swap, preferred_element_type=jnp.float32)
        return (part.astype(jnp.float32) * cosine + swapped * sine).astype(jnp.bfloat16)

    for head in range(heads):
        lanes = slice(128 * head, 128 * head + 128)
        kv_ref[head, :, 0:128] = turned(k_ref, lanes)
        kv_ref[head, :, 128:256] = turned(dk_ref, lanes)
        kv_ref[head, :, 256:384] = v_ref[:, lanes]
        kv_ref[head, :, 384:512] = dv_ref[:, lanes]
        qq_ref[head, :, 0:128] = turned(dq_ref, lanes)
        qq_ref[head, :, 128:256] = turned(q_ref, lanes)


def rotate_all(queries, keys, values, d_queries, d_keys, d_values, positions, key_lists):
    group = 4
    steps = 24 // group
    whole = pl.BlockSpec(memory_space=pltpu.VMEM)
    columns = pl.BlockSpec((CHUNK, 128 * group), lambda i: (0, i))
    return pl.pallas_call(
        rotate_kernel,
        name="rotate",
        grid=(steps,),
        out_shape=(
            jax.ShapeDtypeStruct((24, CHUNK, 512), jnp.bfloat16),
            jax.ShapeDtypeStruct((24, CHUNK, 256), jnp.bfloat16),
            jax.ShapeDtypeStruct((6, 5), jnp.int32),
        ),
        in_specs=[pl.BlockSpec(memory_space=pltpu.SMEM), whole, whole, whole] + [columns] * 6,
        out_specs=(
            pl.BlockSpec((group, CHUNK, 512), lambda i: (i, 0, 0)),
            pl.BlockSpec((group, CHUNK, 256), lambda i: (i, 0, 0)),
            pl.BlockSpec(memory_space=pltpu.SMEM),
        ),
        scratch_shapes=[pltpu.VMEM((CHUNK, 128), jnp.float32)] * 2,
        compiler_params=pltpu.CompilerParams(vmem_limit_bytes=62 * 2**20),
    )(
        key_lists, positions, jnp.asarray(frequency_rows()), jnp.asarray(swap_table(), jnp.bfloat16),
        queries, keys, values, d_queries, d_keys, d_values,
    )


GROUP = 256
KV_WAIT = (SLOTS + 4) * GROUP
Q_PASS, Q_WAIT, Q_ROWS = 3 * QB, 7 * QB, 10 * QB
CODES = [run_code(CHIP_AT[side][x], j) for j in range(3) for side in range(2) for x in range(4)]


def window(x, side, j):
    code = pick(8 * j + 4 * side + x, CODES)
    return code // 4096, (code // 64) % 64, code % 64


def wants(side, block):
    return jnp.where(side == 0, block <= 10, block >= 5)


def kv_place(x, side, j, block):
    low, high, base = window(x, side, j)
    inside = jnp.logical_and(block >= low, block <= high)
    full = 1 if isinstance(j, int) and j == 1 else jnp.where(j == 1, 1, 0)
    return jnp.where(inside, block - low + base, SLOTS + 2 * full + (block // 2) % 2)


def q_place(x, j, block):
    job = 16 * j + block
    full = 1 if isinstance(j, int) and j == 1 else jnp.where(j == 1, 1, 0)
    passing = Q_PASS + (2 * full + (block // 2) % 2) * QB
    return jnp.where(pick(job // 6, CHIP_X) == x, (job % 6) // 2 * QB, passing)


def at_rows(ref, first, count, step):
    return ref.at[pl.ds(pl.multiple_of(first, step), count)]


def at_kv(ref, row, count, step):
    return ref.at[row // GROUP, pl.ds(pl.multiple_of(row % GROUP, step), count)]


def whole_kernel(
    table, pkv, pq, results,
    kv0, kv1, kv2, kv3, qq, out, top, total, light, tilt,
    zs, zqs, ys, yqs, xs, xqs, fs, zr, zqr, yr, yqr, kr, qr, fr, os, done,
):
    quarters = (kv0, kv1, kv2, kv3)
    block, x, y_hi, y_lo, y, z, core = coordinates()
    side = y % 2
    chip = my_chip(x, y)
    always = block >= 0
    no, both = jnp.logical_not, jnp.logical_and

    barrier = pltpu.get_barrier_semaphore()
    partners = (
        [device(x, y, (z + d) % 4, core) for d in (1, 2, 3)]
        + [device(x, (y + d) % 4, z, core) for d in (1, 2, 3)]
        + [device((x + d) % 4, y, z, core) for d in (1, 2, 3)]
        + [device(x, y, z, 1 - core)]
    )
    for partner in partners:
        pl.semaphore_signal(barrier, inc=1, device_id=partner, device_id_type=MESH)
    own = jnp.int32(0)
    for z_from in range(4):
        for g in range(2):
            for j in range(3):
                owner = (16 * j + block) // 6
                x_from, y_from = pick(owner, CHIP_X), 2 * g + owner // 4
                me = both(both(x_from == x, y_from == y), z == z_from)
                own = own + me.astype(jnp.int32)

                @pl.when(no(me))
                def _():
                    pl.semaphore_signal(
                        barrier, inc=1, device_id=device(x_from, y_from, z_from, core), device_id_type=MESH
                    )

    pl.semaphore_wait(barrier, len(partners) + 24 - own)

    draining = []

    def send(where, source, target, send_sem, recv_sem, to):
        remote = pltpu.make_async_remote_copy(
            src_ref=source, dst_ref=target, send_sem=send_sem, recv_sem=recv_sem, device_id=to, device_id_type=MESH
        )

        @pl.when(where)
        def _():
            if draining:
                remote.wait_send()
            else:
                remote.start()

    def keep(source, target, sem):
        if not draining:
            pltpu.make_async_copy(source, target, sem).start()

    def arrived(where, target, recv_sem):
        if draining:
            return

        @pl.when(where)
        def _():
            pltpu.make_async_copy(target, target, recv_sem).wait()


    def kv_after_z(hh, first, size):
        g, j = hh // 3, hh % 3
        stays = both(y_hi == g, side == j // 2 if j != 1 else wants(side, block))
        in_place = kv_place(x, side, j, block) * GROUP + first + y_lo * (size // 2)
        return jnp.where(stays, in_place, KV_WAIT + hh * (GROUP // 2) + first // 2)

    def head_of(place, b):
        return (2 * (place + 3 - (b // 2) % 3)) % 3

    def q_after_z(place, g):
        j = head_of(place, block)
        stays = both(y_hi == g, side == (16 * j + block) // 24)
        row = jnp.where(stays, q_place(x, j, block) + y_lo * 512, Q_WAIT + (3 * g + j) * 512)
        return j, stays, row

    def z_kv(mid, part, start, size):
        kv, first = quarters[start // GROUP], start % GROUP
        for hh in (1, 4) if mid else (0, 5, 2, 3):
            count = size // 8
            to_rows = at_kv(kv, kv_after_z(hh, first, size) + z * count, count, STEP // 8)
            for d in (2, 1, 3, 0):
                to = (z + d) % 4
                from_rows = pkv.at[6 * to + hh, pl.ds(start // 8, count)]
                if d:
                    send(always, from_rows, to_rows, zs.at[hh, part, d], zr.at[hh, part], device(x, y, to, core))
                else:
                    keep(from_rows, to_rows, zr.at[hh, part])

    def z_q(place):
        for g in range(2):
            j, _, row = q_after_z(place, g)
            to_rows = at_rows(qq, row + z * CHUNK, CHUNK, CHUNK)
            for d in (2, 1, 3, 0):
                to = (z + d) % 4
                from_rows = pq.at[6 * to + 3 * g + j]
                if d:
                    send(
                        always, from_rows, to_rows, zqs.at[place, g, d], zqr.at[place, g], device(x, y, to, core)
                    )
                else:
                    keep(from_rows, to_rows, zqr.at[place, g])

    def y_kv(mid, part, start, size):
        kv, first = quarters[start // GROUP], start % GROUP
        count = size // 2
        for hh in (1, 4) if mid else (0, 5, 2, 3):
            g, j = hh // 3, hh % 3
            source = at_kv(kv, kv_after_z(hh, first, size), count, STEP // 2)
            arrived(always, source, zr.at[hh, part])
            for s in (0, 1) if mid else (j // 2,):
                where = wants(jnp.int32(s), block) if mid else always
                to = 2 * g + s
                row = kv_place(x, s, j, block) * GROUP + first + y_lo * count
                send(
                    both(where, y != to), source, at_kv(kv, row, count, STEP // 2),
                    ys.at[hh, s, part], yr.at[mid, y_hi, y_lo, part], device(x, to, z, core),
                )

    def y_q(place):
        for g in range(2):
            j, stays, row = q_after_z(place, g)
            source = at_rows(qq, row, 512, 512)
            arrived(always, source, zqr.at[place, g])
            send(
                no(stays), source, at_rows(qq, q_place(x, j, block) + y_lo * 512, 512, 512),
                yqs.at[place, g], yqr.at[place, y_hi, y_lo], device(x, 2 * g + (16 * j + block) // 24, z, core),
            )

    def x_kv(mid, part, start, size):
        kv, first = quarters[start // GROUP], start % GROUP
        j = 1 if mid else 2 * side
        for t in (0, 1):
            here = 4 * x + 2 * t + core
            came = wants(side, here) if mid else always
            place = kv_place(x, side, j, here)
            row = place * GROUP + first
            for half in (0, 1):
                own = both(t == y_hi, half == y_lo)
                rows = at_kv(kv, row + half * (size // 2), size // 2, STEP // 2)
                arrived(both(came, no(own)), rows, yr.at[mid, t, half, part])
            source = at_kv(kv, row, size, STEP)
            for d in (2, 1, 3):
                to = (x + d) % 4
                low, high, base = window(to, side, j)
                wanted = both(here >= low, here <= high)
                slot = jnp.where(wanted, here - low + base, 0)
                send(
                    wanted, source, at_kv(kv, slot * GROUP + first, size, STEP),
                    xs.at[mid, t, d, part], kr.at[slot, part], device(to, y, z, core),
                )
            kept = both(came, place < SLOTS)
            slot = jnp.where(kept, place, 0)
            rows = at_kv(kv, slot * GROUP + first, size, STEP)
            send(kept, rows, rows, fs.at[mid, t, 0, part], fr.at[slot, part], device(x, y, z, 1 - core))

    def x_q(place):
        for t in (0, 1):
            here = 4 * x + 2 * t + core
            j = head_of(place, here)
            job = 16 * j + here
            owned = job // 24 == side
            row = q_place(x, j, here)
            for half in (0, 1):
                own = both(t == y_hi, half == y_lo)
                arrived(both(owned, no(own)), at_rows(qq, row + half * 512, 512, 512), yqr.at[place, t, half])
            to = pick(job // 6, CHIP_X)
            send(
                both(owned, to != x), at_rows(qq, row, QB, QB), at_rows(qq, place * QB, QB, QB),
                xqs.at[place, t], qr.at[place], device(to, y, z, core),
            )

    def wanted_here(mid, t, d, other):
        low, high, base = window(x, side, 1 if mid else 2 * side)
        from_block = 4 * ((x + d) % 4) + 2 * t + (1 - core if other else core)
        wanted = both(from_block >= low, from_block <= high)
        return wanted, jnp.where(wanted, from_block - low + base, 0)

    def to_other_core(mid, part, start, size):
        kv, first = quarters[start // GROUP], start % GROUP
        for d in (1, 3, 2):
            for t in (0, 1):
                wanted, slot = wanted_here(mid, t, d, False)
                rows = at_kv(kv, slot * GROUP + first, size, STEP)
                arrived(wanted, rows, kr.at[slot, part])
                send(wanted, rows, rows, fs.at[mid, t, d, part], fr.at[slot, part], device(x, y, z, 1 - core))

    stages = {"z": z_kv, "y": y_kv, "x": x_kv, "c": to_other_core}
    stages_q = {"z": z_q, "y": y_q, "x": x_q}

    def go(step):
        name, item = step
        if isinstance(item, tuple):
            for mid in (0, 1):
                stages[name](mid, *item)
        else:
            stages_q[name](item)

    def complete(part, start, size):
        kv, first = quarters[start // GROUP], start % GROUP
        for mid, t in ((0, 0), (0, 1), (1, 0), (1, 1)):
            for d in (0, 1, 3, 2):
                wanted, slot = wanted_here(mid, t, d, True)
                arrived(wanted, at_kv(kv, slot * GROUP + first, size, STEP), fr.at[slot, part])

    def attend(quarter, i):
        at = pl.ds(pl.multiple_of(i * QB, QB), QB)
        kv = quarters[quarter]
        held = [kv[table[i, s]] for s in range(5)]
        absent = [jnp.where(table[3 + i, s] == 1, 0.0, 1e32) for s in range(5)]
        both_keys = jnp.concatenate([block_rows[:, 0:256] for block_rows in held], axis=0)
        both_values = jnp.concatenate([block_rows[:, 256:512] for block_rows in held], axis=0)
        ones = jnp.ones((5 * GROUP, 128), jnp.bfloat16)
        values = jnp.concatenate([both_values[:, 0:128], ones], axis=1)
        across = (((1,), (1,)), ((), ()))
        rows = qq[at, :]
        score = lax.dot_general(
            rows[:, 128:256], both_keys[:, 0:128], across, preferred_element_type=jnp.float32
        )
        d_score = lax.dot_general(rows, both_keys, across, preferred_element_type=jnp.float32)
        parts = [score[:, s * GROUP : (s + 1) * GROUP] for s in range(5)]
        tops = [jnp.max(parts[s], axis=1, keepdims=True) - absent[s] for s in range(5)]
        peak = functools.reduce(jnp.maximum, tops)
        if quarter:
            old = top[at, :]
            new = jnp.maximum(old, peak)
            fade = jnp.exp2((old - new) * (SCALE * LOG2E))
            fade2 = jnp.concatenate([fade, fade], axis=1)
        else:
            new = jnp.broadcast_to(peak, (QB, 128))
        weight = jnp.concatenate(
            [jnp.exp2((parts[s] - (new[:, 0:1] + absent[s])) * (SCALE * LOG2E)) for s in range(5)], axis=1
        )
        tilted = weight * d_score
        sums = weight[:, 0:128]
        for c in range(1, 5 * GROUP // 128):
            sums = sums + weight[:, 128 * c : 128 * c + 128]
        lit = jnp.dot(weight.astype(jnp.bfloat16), both_values, preferred_element_type=jnp.float32)
        leaned = jnp.dot(tilted.astype(jnp.bfloat16), values, preferred_element_type=jnp.float32)
        if quarter:
            sums = total[at, :] * fade + sums
            lit = light[at, :] * fade2 + lit
            leaned = tilt[at, :] * fade2 + leaned
        if quarter < 3:
            top[at, :] = new
            total[at, :] = sums
            light[at, :] = lit
            tilt[at, :] = leaned
        else:
            inverse = 1.0 / jnp.sum(sums, axis=1, keepdims=True)
            result = lit[:, 0:128] * inverse
            moved = lit[:, 128:256] + SCALE * leaned[:, 0:128]
            slope = SCALE * leaned[:, 128:256]
            out[at, 0:128] = result.astype(jnp.bfloat16)
            out[at, 128:256] = (moved * inverse - slope * inverse * result).astype(jnp.bfloat16)

    def give_back(i):
        job = 6 * chip + 2 * i + core
        j, b = job // 16, job % 16
        head = 6 * z + 3 * (y // 2) + j
        for d in range(8):
            p = (d + 4 * y_lo + z) % 8
            me = both(b == block, p == 4 * y_lo + z)
            from_ref, to_ref = at_rows(out, i * QB + p * CHUNK, CHUNK, CHUNK), results.at[head]
            if not draining:

                @pl.when(me)
                def _():
                    pltpu.make_async_copy(from_ref, to_ref, done).start()

            send(no(me), from_ref, to_ref, os.at[i, d], done, (b, p))

    first, between = PROGRAM
    for step in first:
        go(step)

    @pl.loop(0, 3)
    def _(i):
        b = (6 * chip + 2 * i + core) % 16
        arrived(b // 4 != x, at_rows(qq, i * QB, QB, QB), qr.at[i])
        for quarter in range(4):

            @pl.when(i == 0)
            def _():
                for step in between[quarter]:
                    go(step)
                for part, start, size in PARTS:
                    if start // GROUP == quarter:
                        complete(part, start, size)

            attend(quarter, i)
        give_back(i)

    pltpu.make_async_copy(results, results, done).wait()
    draining.append(True)
    for step in first + between[0] + between[1] + between[2] + between[3]:
        go(step)

    @pl.loop(0, 3)
    def _(i):
        give_back(i)


STEP = 128
SIZES = (128, 128, 256, 256, 256)
PARTS = [(part, sum(SIZES[:part]), size) for part, size in enumerate(SIZES)]


def make_program(order, lead, lag_x, lag_c, before, where):
    steps = [PARTS[int(c)] if c.isdigit() else "abc".index(c) for c in order]

    def one(stage, index):
        if not 0 <= index < len(steps) or (stage == "c" and not isinstance(steps[index], tuple)):
            return []
        return [(stage, steps[index])]

    first = [step for i in range(lead) for step in one("z", i)]
    turns = [
        one("y", turn) + one("z", turn + lead) + one("x", turn - lag_x) + one("c", turn - lag_c)
        for turn in range(len(steps) + max(lag_x, lag_c))
    ]
    for turn in turns[:before]:
        first += turn
    between = [[] for _ in range(4)]
    for place, turn in zip(where, turns[before:]):
        between[place] += turn
    return first, between


PROGRAM = make_program("0123a4bc", 3, 1, 3, 6, (1, 2, 3))


def bring_attend_return(table, pkv, pq):
    anywhere = pl.BlockSpec(memory_space=pl.ANY)
    dma, vmem = pltpu.SemaphoreType.DMA, pltpu.VMEM
    n = len(PARTS)
    sems = [
        (6, n, 4), (3, 2, 4), (6, 2, n), (3, 2), (2, 2, 4, n), (3, 2), (2, 2, 4, n),
        (6, n), (3, 2), (2, 2, 2, n), (3, 2, 2), (SLOTS, n), (3,), (SLOTS, n), (3, 8),
    ]
    return pl.pallas_call(
        whole_kernel,
        name="bring_attend_return",
        out_shape=jax.ShapeDtypeStruct((24, CHUNK, 256), jnp.bfloat16),
        in_specs=[pl.BlockSpec(memory_space=pltpu.SMEM), anywhere, anywhere],
        out_specs=anywhere,
        scratch_shapes=[vmem((SLOTS + 7, GROUP, 512), jnp.bfloat16)] * 4
        + [vmem((Q_ROWS, 256), jnp.bfloat16)]
        + [vmem((3 * QB, 256), jnp.bfloat16)]
        + [vmem((3 * QB, 128), jnp.float32)] * 2
        + [vmem((3 * QB, 256), jnp.float32)] * 2
        + [dma(shape) for shape in sems]
        + [dma],
        compiler_params=pltpu.CompilerParams(
            collective_id=0, has_side_effects=True, vmem_limit_bytes=62 * 2**20
        ),
    )(table, pkv, pq)


def on_device(queries, keys, values, d_queries, d_keys, d_values, positions, key_lists):
    pkv, pq, table = rotate_all(queries, keys, values, d_queries, d_keys, d_values, positions, key_lists)
    by_head = bring_attend_return(table, pkv, pq)
    return tuple(
        by_head[:, :, first : first + 128].transpose(1, 0, 2).reshape(CHUNK, 3072) for first in (0, 128)
    )


def solution(mesh):
    tokens = P(("blk", "head"), None)
    return jax.shard_map(
        on_device,
        mesh=mesh,
        in_specs=(tokens,) * 6 + (P(None, ("blk", "head")), P()),
        out_specs=(tokens, tokens),
        check_vma=False,
    )
```
